128 devices in a mesh: seq: 16 (over x, y), head: 8 (over z, core).
Axes of the slice: x: 4, y: 4, z: 4, core: 2. Of those that a mesh axis runs over, the one named last changes fastest.
Arguments:
- node_input: bfloat16 [49152, 1024], P(('seq', 'head')), may hold values from -13 to 13
- w_query: bfloat16 [1024, 1024], P(None, 'head'), may hold values from -0.1875 to 0.1875
- w_key: bfloat16 [1024, 1024], P(None, 'head'), may hold values from -0.1875 to 0.1875
- w_value: bfloat16 [1024, 1024], P(None, 'head'), may hold values from -0.1875 to 0.1875
- grad_context: bfloat16 [49152, 1024], P(('seq', 'head')), may hold values from -6 to 6
- key_blocks: int32 [384, 4], P('seq'), may hold values from 0 to 383, as said below
- counts: int32 [384], P('seq'), may hold values from 1 to 4
Outputs:
- grad_input: bfloat16 [49152, 1024], P(('seq', 'head'))
- grad_wq: float32 [1024, 1024], P('seq', 'head')
- grad_wk: float32 [1024, 1024], P('seq', 'head')
- grad_wv: float32 [1024, 1024], P('seq', 'head')
The draws below stay inside these ranges and needn't reach their ends.
Inputs may be any that keep to these rules, and one draw needn't show every extreme that they name: `key_blocks`: entry 0 of the list of block b is b itself. Block g is owned by seq index g // 24. Among entries 1 to 3 of the lists of the 24 blocks of one seq index, at most 7 name blocks of any one owner; in every draw one owner is named exactly 7 times by every seq index. Entries may repeat.
All inputs are finite; a program needn't handle non-finite values.
Results may differ from the reference program's by a relative error of at most 0.006.
The reference program's roundings to bfloat16 on the way (of `grad_query`) count: a program that leaves them out, or rounds other values in their place, can miss the bound.
Values may be sent and summed in bfloat16 or wider, within the bound.
No kernel may reach another device: no remote copies, remote signals or barrier semaphores. Data moves between devices by JAX's collectives and lax.ppermute only.
A program may use at most 128 MiB of HBM per device.

```python
import jax
import jax.numpy as jnp
from jax import lax

D = 1024
HEADS = 16
HDIM = 64
BLOCK = 128
KB = 4
NB_DEV = 24
NBLK = 384
NODES = 49152
CAP = 7
N_SEQ = 16


def draw_node_input(key, part):
    key = jax.random.fold_in(key, 5)
    base_key = jax.random.fold_in(key, 0)
    return jax.random.truncated_normal(base_key, -6.0, 6.0, (NODES, D), jnp.float32).astype(jnp.bfloat16)


def draw_key_blocks(key, part):
    key = jax.random.fold_in(key, 11)
    hot_key, rest_key = jax.random.split(key)
    hot_owner = jax.random.randint(hot_key, (), 0, N_SEQ)
    remote = NB_DEV * (KB - 1)
    pool_size = N_SEQ * CAP

    def one_device(device_key):
        perm_key, shuffle_key, pick_key = jax.random.split(device_key, 3)
        owners = jax.random.permutation(perm_key, pool_size) // CAP
        sort_score = jnp.where(owners == hot_owner, 0, 1) * pool_size + jnp.arange(pool_size)
        pool_order = jnp.argsort(sort_score)
        chosen = owners[pool_order][:remote]
        chosen = chosen[jax.random.permutation(shuffle_key, remote)]
        inner_block = jax.random.randint(pick_key, (remote,), 0, NB_DEV)
        return (chosen * NB_DEV + inner_block).reshape(NB_DEV, KB - 1)
    remote_lists = jax.vmap(one_device)(jax.random.split(rest_key, N_SEQ))
    own_blocks = jnp.arange(N_SEQ * NB_DEV).reshape(N_SEQ, NB_DEV, 1)
    joined = jnp.concatenate([own_blocks, remote_lists], axis=2)
    return joined.reshape(N_SEQ * NB_DEV, KB).astype(jnp.int32)


def set_ends(entries, rng, smallest, high):
    longest = entries.shape.index(max(entries.shape))
    spots = []
    for shift in (0, 1):
        where = [jax.random.randint(jax.random.fold_in(rng, axis), (), 0, length) for axis, length in enumerate(entries.shape)]
        where[longest] = (where[longest] + shift) % entries.shape[longest]
        spots.append(tuple(where))
    return entries.at[spots[0]].set(smallest).at[spots[1]].set(high)


def block_levels(rng, dims, pieces, low, largest):
    factor_of = 1.0
    for dim, parts in pieces:
        draws = jax.random.uniform(jax.random.fold_in(jax.random.fold_in(rng, 6), dim), (parts,), jnp.float32, low / len(pieces), largest / len(pieces))
        factor_of = factor_of * jnp.repeat(jnp.exp(draws), dims[dim] // parts).reshape((-1,) + (1,) * (len(dims) - 1 - dim))
    return factor_of


def normal_values(key, extent, scale, reach, pieces=(), held_as=jnp.bfloat16):
    factor_of = block_levels(key, extent, pieces, -0.22, 0.18) if pieces else 1.0
    result = jax.random.normal(key, extent, jnp.float32) * scale * factor_of
    return jnp.minimum(jnp.maximum(result, -reach), reach).astype(held_as)


def setup_inputs(seed: int = 0) -> dict:
    key_list = jax.random.split(jax.random.key(seed), 8)
    node_input = draw_node_input(jax.random.fold_in(key_list[7], 71), 0)
    w_query = normal_values(key_list[1], (D, D), D ** -0.5, 0.1875, ((1, 8),))
    w_key = normal_values(key_list[2], (D, D), D ** -0.5, 0.1875, ((1, 8),))
    w_value = normal_values(key_list[3], (D, D), D ** -0.5, 0.1875, ((1, 8),))
    grad_context = normal_values(key_list[4], (NODES, D), 1.0, 6.0, ((0, 128),))
    key_blocks = draw_key_blocks(jax.random.fold_in(key_list[7], 71), 0)
    counts = set_ends(jax.random.randint(key_list[6], (NBLK,), 1, KB + 1), jax.random.fold_in(key_list[6], 1), 1, KB).astype(jnp.int32)
    return {"node_input": node_input, "w_query": w_query, "w_key": w_key, "w_value": w_value, "grad_context": grad_context, "key_blocks": key_blocks, "counts": counts}


def round_far(terms):
    near = terms[:1]
    far = lax.optimization_barrier(terms[1:].astype(jnp.bfloat16)).astype(jnp.float32)
    return jnp.concatenate([near, far], axis=0)


def reference(node_input, w_query, w_key, w_value, grad_context, key_blocks, counts):
    queries = jnp.dot(node_input, w_query, preferred_element_type=jnp.float32).astype(jnp.bfloat16)
    keys_all = jnp.dot(node_input, w_key, preferred_element_type=jnp.float32).astype(jnp.bfloat16)
    values_all = jnp.dot(node_input, w_value, preferred_element_type=jnp.float32).astype(jnp.bfloat16)
    blocks = NODES // BLOCK
    softmax_scale = HDIM ** -0.5
    query_tiles = queries.reshape(blocks, BLOCK, HEADS, HDIM)
    key_tiles = keys_all.reshape(blocks, BLOCK, HEADS, HDIM)
    value_tiles = values_all.reshape(blocks, BLOCK, HEADS, HDIM)
    grad_tiles = grad_context.reshape(blocks, BLOCK, HEADS, HDIM)

    def one_block(carry, block_index):
        key_grads, value_grads = carry
        listed = key_blocks[block_index]
        valid_entry = jnp.arange(KB, dtype=jnp.int32) < counts[block_index]
        keep_mask = valid_entry[None, None, :, None]
        query_now = query_tiles[block_index].astype(jnp.float32)
        grad_now = grad_tiles[block_index].astype(jnp.float32)
        key_set = key_tiles[listed].astype(jnp.float32)
        value_set = value_tiles[listed].astype(jnp.float32)
        scores = jnp.einsum("qhd,jkhd->hqjk", query_now, key_set) * softmax_scale
        row_max = jnp.max(jnp.where(keep_mask, scores, -1e30), axis=(2, 3), keepdims=True)
        unnorm = jnp.where(keep_mask, jnp.exp(scores - row_max), 0.0)
        probs = unnorm / jnp.sum(unnorm, axis=(2, 3), keepdims=True)
        grad_probs = jnp.einsum("qhd,jkhd->hqjk", grad_now, value_set)
        delta_rows = jnp.sum(probs * grad_probs, axis=(2, 3), keepdims=True)
        grad_scores = (probs * (grad_probs - delta_rows) * softmax_scale).astype(jnp.bfloat16)
        probs_low = probs.astype(jnp.bfloat16)
        grad_scores = lax.optimization_barrier(grad_scores).astype(jnp.float32)
        probs_low = lax.optimization_barrier(probs_low).astype(jnp.float32)
        query_grad = jnp.einsum("hqjk,jkhd->qhd", grad_scores, key_set).astype(jnp.bfloat16)
        part_keys = round_far(jnp.einsum("hqjk,qhd->jkhd", grad_scores, query_now).reshape(KB, BLOCK, D))
        part_values = round_far(jnp.einsum("hqjk,qhd->jkhd", probs_low, grad_now).reshape(KB, BLOCK, D))
        key_grads = key_grads.at[listed].add(part_keys)
        value_grads = value_grads.at[listed].add(part_values)
        return (key_grads, value_grads), query_grad.reshape(BLOCK, D)

    empty = jnp.zeros((blocks, BLOCK, D), jnp.float32)
    (key_grads, value_grads), query_grads = lax.scan(one_block, (empty, empty), jnp.arange(blocks, dtype=jnp.int32))
    grad_query = query_grads.reshape(NODES, D)
    grad_key = key_grads.reshape(NODES, D).astype(jnp.bfloat16)
    grad_value = value_grads.reshape(NODES, D).astype(jnp.bfloat16)
    summed = jnp.dot(grad_query, w_query.T, preferred_element_type=jnp.float32)
    summed = summed + jnp.dot(grad_key, w_key.T, preferred_element_type=jnp.float32)
    summed = summed + jnp.dot(grad_value, w_value.T, preferred_element_type=jnp.float32)
    grad_input = summed.astype(jnp.bfloat16)
    grad_wq = jnp.dot(node_input.T, grad_query, preferred_element_type=jnp.float32)
    grad_wk = jnp.dot(node_input.T, grad_key, preferred_element_type=jnp.float32)
    grad_wv = jnp.dot(node_input.T, grad_value, preferred_element_type=jnp.float32)
    return grad_input, grad_wq, grad_wk, grad_wv
```

```python
import functools

import jax
import jax.numpy as jnp
from jax import lax
from jax.experimental import pallas as pl
from jax.experimental.pallas import tpu as pltpu
from jax.sharding import PartitionSpec as P

HDIM = 64
BLOCK = 128
KB = 4
BF16 = jnp.bfloat16
F32 = jnp.float32
SCALE = HDIM ** (-0.5)
GROUP = 4
VMEM_LIMIT = 48 * 1024 * 1024
VMEM = pl.BlockSpec(memory_space=pltpu.VMEM)
SMEM = pl.BlockSpec(memory_space=pltpu.SMEM)
NT = (((1,), (1,)), ((), ()))
TN = (((0,), (0,)), ((), ()))


def params():
    return pltpu.CompilerParams(vmem_limit_bytes=VMEM_LIMIT)


def cost(flops, moved):
    return pl.CostEstimate(flops=int(flops), bytes_accessed=int(moved), transcendentals=0)


def head_mask(width):
    heads = width // HDIM
    row_head = jnp.arange(heads * BLOCK)[:, None] // BLOCK
    col_head = jnp.arange(width)[None, :] // HDIM
    return (row_head == col_head).astype(BF16)


def by_head(tile, mask_ref):
    heads = mask_ref.shape[0] // BLOCK
    return jnp.concatenate([tile] * heads, axis=0) * mask_ref[...]


def listed(meta_ref, order_ref, total):
    def scan(i, n):
        wanted = meta_ref[i] >= 0

        @pl.when(wanted)
        def _():
            order_ref[n] = i

        return n + wanted.astype(jnp.int32)

    return lax.fori_loop(0, total, scan, 0)


def row_stats(key_heads, value_heads, query, grad):
    heads = key_heads.shape[0] // BLOCK
    scores = lax.dot_general(key_heads, query, NT, preferred_element_type=F32)
    grad_probs = lax.dot_general(value_heads, grad, NT, preferred_element_type=F32)
    scores = scores.reshape(heads, BLOCK, BLOCK)
    grad_probs = grad_probs.reshape(heads, BLOCK, BLOCK)
    top = jnp.max(scores, axis=1, keepdims=True)
    unnorm = jnp.exp((scores - top) * SCALE)
    total = jnp.sum(unnorm, axis=1)
    weighted = jnp.sum(unnorm * grad_probs, axis=1)
    return top[:, 0] * SCALE + jnp.log(total), weighted / total


def slot_rows(ref, slot, per):
    return ref[slot // per, pl.ds(lax.rem(slot, per) * BLOCK, BLOCK), :]


def remote_stats_kernel(per, meta_ref, query_ref, grad_ref, key_ref, value_ref, mask_ref, out_ref, order_ref):
    total = meta_ref.shape[0]
    heads = mask_ref.shape[0] // BLOCK
    out_ref[...] = jnp.zeros_like(out_ref)
    n = listed(meta_ref, order_ref, total)

    def step(g, carry):
        for u in range(GROUP):
            slot = order_ref[jnp.minimum(g * GROUP + u, n - 1)]
            block = meta_ref[slot]
            lse, delta = row_stats(
                by_head(key_ref[block], mask_ref),
                by_head(value_ref[block], mask_ref),
                slot_rows(query_ref, slot, per),
                slot_rows(grad_ref, slot, per),
            )
            out_ref[slot, 0:heads] = lse
            out_ref[slot, heads : 2 * heads] = delta
        return carry

    lax.fori_loop(0, pl.cdiv(n, GROUP), step, 0)


def own_stats_kernel(query_ref, grad_ref, key_ref, value_ref, mask_ref, out_ref):
    heads = mask_ref.shape[0] // BLOCK
    blocks = query_ref.shape[0]

    def step(g, carry):
        for u in range(GROUP):
            b = g * GROUP + u
            lse, delta = row_stats(
                by_head(key_ref[b], mask_ref),
                by_head(value_ref[b], mask_ref),
                query_ref[b],
                grad_ref[b],
            )
            out_ref[b, 0:heads] = lse
            out_ref[b, heads : 2 * heads] = delta
        return carry

    lax.fori_loop(0, blocks // GROUP, step, 0)


def merge_kernel(slot_ref, count_ref, own_ref, far_ref, row_ref, back_ref, lse_ref, delta_ref):
    blocks = own_ref.shape[0]
    heads = own_ref.shape[1] // 2
    back_ref[...] = jnp.zeros_like(back_ref)
    for b in range(blocks):
        for j in range(KB - 1):
            live = count_ref[b] > j + 1
            stats = far_ref[slot_ref[b * (KB - 1) + j]]
            lse_ref[j, b] = jnp.where(live, stats[:heads], -1e30)
            delta_ref[j, b] = jnp.where(live, stats[heads:], 0.0)
    own = own_ref[...]
    lses = [own[:, :heads]] + [lse_ref[j] for j in range(KB - 1)]
    deltas = [own[:, heads:]] + [delta_ref[j] for j in range(KB - 1)]
    top = functools.reduce(jnp.maximum, lses)
    weights = [jnp.exp(v - top) for v in lses]
    total = sum(weights)
    row_ref[:, :heads] = top + jnp.log(total)
    row_ref[:, heads:] = sum(w * d for w, d in zip(weights, deltas)) / total
    for b in range(blocks):
        for j in range(KB - 1):
            back_ref[slot_ref[b * (KB - 1) + j]] = row_ref[b]


def entry_grads(key_heads, value_heads, query, grad, stats):
    heads = key_heads.shape[0] // BLOCK
    scores = lax.dot_general(key_heads, query, NT, preferred_element_type=F32)
    grad_probs = lax.dot_general(value_heads, grad, NT, preferred_element_type=F32)
    scores = scores.reshape(heads, BLOCK, BLOCK)
    grad_probs = grad_probs.reshape(heads, BLOCK, BLOCK)
    probs = jnp.exp(scores * SCALE - stats[:heads][:, None, :])
    grad_scores = probs * (grad_probs - stats[heads:][:, None, :]) * SCALE
    flat = (heads * BLOCK, BLOCK)
    return probs.astype(BF16).reshape(flat), grad_scores.astype(BF16).reshape(flat)


def pick_heads(stacked):
    width = stacked.shape[1]
    heads = width // HDIM
    col_head = lax.broadcasted_iota(jnp.int32, (BLOCK, width), 1) // HDIM
    picked = stacked[:BLOCK]
    for h in range(1, heads):
        picked = jnp.where(col_head == h, stacked[h * BLOCK : (h + 1) * BLOCK], picked)
    return picked


def far_query_kernel(per, meta_ref, query_ref, grad_ref, stats_ref, key_ref, value_ref, mask_ref, out_ref, order_ref):
    total = meta_ref.shape[0]
    n = listed(meta_ref, order_ref, total)

    def step(g, carry):
        for u in range(GROUP):
            slot = order_ref[jnp.minimum(g * GROUP + u, n - 1)]
            block = meta_ref[slot]
            key_heads = by_head(key_ref[block], mask_ref)
            _, grad_scores = entry_grads(
                key_heads,
                by_head(value_ref[block], mask_ref),
                slot_rows(query_ref, slot, per),
                slot_rows(grad_ref, slot, per),
                stats_ref[slot],
            )
            term = lax.dot_general(grad_scores, key_heads, TN, preferred_element_type=F32)
            out_ref[slot] = term.astype(BF16)
        return carry

    lax.fori_loop(0, pl.cdiv(n, GROUP), step, 0)


def key_value_kernel(
    per,
    meta_ref,
    far_query_ref,
    far_grad_ref,
    far_stats_ref,
    query_ref,
    grad_ref,
    stats_ref,
    key_ref,
    value_ref,
    mask_ref,
    own_term_ref,
    key_out_ref,
    value_out_ref,
    order_ref,
    key_sum,
    value_sum,
):
    blocks = query_ref.shape[0]
    total = meta_ref.shape[0]

    def own(g, carry):
        for u in range(GROUP):
            b = g * GROUP + u
            key_heads = by_head(key_ref[b], mask_ref)
            query = query_ref[b]
            grad = grad_ref[b]
            probs, grad_scores = entry_grads(
                key_heads, by_head(value_ref[b], mask_ref), query, grad, stats_ref[b]
            )
            own_term_ref[b] = lax.dot_general(grad_scores, key_heads, TN, preferred_element_type=F32)
            key_sum[b] = pick_heads(jnp.dot(grad_scores, query, preferred_element_type=F32))
            value_sum[b] = pick_heads(jnp.dot(probs, grad, preferred_element_type=F32))
        return carry

    lax.fori_loop(0, blocks // GROUP, own, 0)
    n = listed(meta_ref, order_ref, total)

    def far(g, carry):
        for u in range(GROUP):
            at = g * GROUP + u
            slot = order_ref[jnp.minimum(at, n - 1)]
            block = meta_ref[slot]
            query = slot_rows(far_query_ref, slot, per)
            grad = slot_rows(far_grad_ref, slot, per)
            probs, grad_scores = entry_grads(
                by_head(key_ref[block], mask_ref),
                by_head(value_ref[block], mask_ref),
                query,
                grad,
                far_stats_ref[slot],
            )
            keep = at < n
            key_term = pick_heads(jnp.dot(grad_scores, query, preferred_element_type=F32))
            value_term = pick_heads(jnp.dot(probs, grad, preferred_element_type=F32))
            key_sum[block] += jnp.where(keep, key_term, 0.0)
            value_sum[block] += jnp.where(keep, value_term, 0.0)
        return carry

    lax.fori_loop(0, pl.cdiv(n, GROUP), far, 0)
    key_out_ref[...] = key_sum[...].astype(BF16)
    value_out_ref[...] = value_sum[...].astype(BF16)


def query_sum_kernel(slot_ref, count_ref, own_ref, far_ref, out_ref):
    blocks = own_ref.shape[0]

    def step(b, carry):
        total = own_ref[b]
        for j in range(KB - 1):
            term = far_ref[slot_ref[b * (KB - 1) + j]].astype(F32)
            total = total + jnp.where(count_ref[b] > j + 1, term, 0.0)
        out_ref[b] = total.astype(BF16)
        return carry

    lax.fori_loop(0, blocks, step, 0)


def pack_kernel(per, peers_step, source_ref, tile_ref, out_ref):
    first = pl.program_id(0) * peers_step
    for p in range(peers_step):
        for r in range(per):
            out_ref[p, r * BLOCK : (r + 1) * BLOCK, :] = tile_ref[source_ref[(first + p) * per + r]]


def pack_meta_kernel(per, peers_step, source_ref, tile_ref, meta_ref, out_ref):
    pack_kernel(per, peers_step, source_ref, tile_ref, out_ref)
    out_ref[:, per * BLOCK :, :] = meta_ref[...]


def pack(tiles, source, meta, n_seq, per):
    blocks, _, cols = tiles.shape
    peers_step = 4
    extra = 0 if meta is None else meta.shape[1]
    rows = per * BLOCK + extra
    in_specs = [pl.BlockSpec((blocks, BLOCK, cols), lambda i, s: (0, 0, 0))]
    operands = [tiles]
    if meta is not None:
        in_specs.append(pl.BlockSpec((peers_step, extra, cols), lambda i, s: (i, 0, 0)))
        operands.append(meta)
    return pl.pallas_call(
        functools.partial(pack_kernel if meta is None else pack_meta_kernel, per, peers_step),
        grid_spec=pltpu.PrefetchScalarGridSpec(
            num_scalar_prefetch=1,
            grid=(n_seq // peers_step,),
            in_specs=in_specs,
            out_specs=pl.BlockSpec((peers_step, rows, cols), lambda i, s: (i, 0, 0)),
        ),
        out_shape=jax.ShapeDtypeStruct((n_seq, rows, cols), BF16),
        compiler_params=params(),
        cost_estimate=cost(0, 2 * 2 * n_seq * rows * cols),
    )(source, *operands)


def seq_exchange(x):
    return lax.all_to_all(x, "seq", split_axis=0, concat_axis=0, tiled=True)


def head_exchange(x):
    n_head = lax.axis_size("head")
    me = lax.axis_index("head")
    parts = x.reshape(n_head, x.shape[0] // n_head, x.shape[1])
    out = []
    for shift in range(n_head):
        chunk = lax.dynamic_index_in_dim(parts, lax.rem(me + shift, n_head), 0, keepdims=False)
        if shift:
            chunk = lax.ppermute(chunk, "head", [(h, (h + shift) % n_head) for h in range(n_head)])
        out.append(chunk)
    return jnp.concatenate(out, axis=1)


def shards(node_input, w_query, w_key, w_value, grad_context, key_blocks, counts):
    n_seq = lax.axis_size("seq")
    n_head = lax.axis_size("head")
    me = lax.axis_index("head")
    cols = w_query.shape[1]
    heads = cols // HDIM
    blocks = key_blocks.shape[0]
    nodes = blocks * BLOCK
    per = max(2, 3 * blocks * (KB - 1) // (2 * n_seq) + 1)
    slots = n_seq * per
    mask = head_mask(cols)

    remote = key_blocks[:, 1:].reshape(-1)
    entries = remote.shape[0]
    owner = remote // blocks
    inner = remote % blocks
    numbers = jnp.arange(entries, dtype=jnp.int32)
    live = (numbers % (KB - 1)) + 1 < counts[numbers // (KB - 1)]
    before = (owner[:, None] == owner[None, :]) & (numbers[None, :] < numbers[:, None])
    slot_of = owner * per + jnp.sum(before.astype(jnp.int32), axis=1)
    taken = slot_of[None, :] == jnp.arange(slots, dtype=jnp.int32)[:, None]
    source = jnp.sum(jnp.where(taken, numbers[None, :] // (KB - 1), 0), axis=1)
    asked = jnp.sum(jnp.where(taken & live[None, :], inner[None, :] + 1, 0), axis=1) - 1
    meta = jnp.broadcast_to(
        jnp.pad(asked.reshape(n_seq, per), ((0, 0), (0, 16 - per)))[:, :, None], (n_seq, 16, cols)
    ).astype(BF16)

    upstream = lax.all_to_all(grad_context, "head", split_axis=1, concat_axis=0, tiled=True)
    grad_tiles = upstream.reshape(blocks, BLOCK, cols)
    far_grads = seq_exchange(pack(grad_tiles, source, meta, n_seq, per))
    far_meta = far_grads[:, per * BLOCK : per * BLOCK + per, 0].astype(jnp.int32).reshape(-1)

    gathered = lax.all_gather(node_input, "head", axis=0, tiled=True)
    queries = jnp.dot(gathered, w_query, preferred_element_type=F32).astype(BF16)
    query_tiles = queries.reshape(blocks, BLOCK, cols)
    far_queries = seq_exchange(pack(query_tiles, source, None, n_seq, per))
    keys = jnp.dot(gathered, w_key, preferred_element_type=F32).astype(BF16)
    values = jnp.dot(gathered, w_value, preferred_element_type=F32).astype(BF16)
    key_tiles = keys.reshape(blocks, BLOCK, cols)
    value_tiles = values.reshape(blocks, BLOCK, cols)

    w_all = jnp.concatenate([w_query, w_key, w_value], axis=0)
    w_all, _ = lax.optimization_barrier((w_all, gathered))
    w_all = lax.all_gather(w_all, "head", axis=0)
    turn = lax.rem(me - jnp.arange(n_head, dtype=jnp.int32) + n_head, n_head)
    w_all = w_all[turn].reshape(n_head, 3, w_query.shape[0], cols)
    w_all = w_all.transpose(1, 2, 0, 3).reshape(3, w_query.shape[0], n_head * cols)

    unit_flops = 2 * heads * BLOCK * BLOCK * cols
    tile_bytes = 2 * BLOCK * cols
    stats_shape = jax.ShapeDtypeStruct((slots, 2 * heads, BLOCK), F32)
    own_stats = pl.pallas_call(
        own_stats_kernel,
        out_shape=jax.ShapeDtypeStruct((blocks, 2 * heads, BLOCK), F32),
        in_specs=[VMEM] * 5,
        out_specs=VMEM,
        compiler_params=params(),
        cost_estimate=cost(2 * blocks * unit_flops, 4 * blocks * tile_bytes),
    )(query_tiles, grad_tiles, key_tiles, value_tiles, mask)
    far_stats = pl.pallas_call(
        functools.partial(remote_stats_kernel, per),
        out_shape=stats_shape,
        in_specs=[SMEM] + [VMEM] * 5,
        out_specs=VMEM,
        scratch_shapes=[pltpu.SMEM((slots,), jnp.int32)],
        compiler_params=params(),
        cost_estimate=cost(2 * slots * unit_flops, 2 * slots * tile_bytes),
    )(far_meta, far_queries, far_grads, key_tiles, value_tiles, mask)
    row_stats_all, back = pl.pallas_call(
        merge_kernel,
        out_shape=(jax.ShapeDtypeStruct((blocks, 2 * heads, BLOCK), F32), stats_shape),
        in_specs=[SMEM, SMEM, VMEM, VMEM],
        out_specs=(VMEM, VMEM),
        scratch_shapes=[pltpu.VMEM((KB - 1, blocks, heads, BLOCK), F32)] * 2,
        compiler_params=params(),
        cost_estimate=cost(0, 2 * 2 * slots * 4 * heads * BLOCK),
    )(slot_of, counts, own_stats, seq_exchange(far_stats))
    back = seq_exchange(back)

    far_terms = pl.pallas_call(
        functools.partial(far_query_kernel, per),
        out_shape=jax.ShapeDtypeStruct((slots, BLOCK, cols), BF16),
        in_specs=[SMEM] + [VMEM] * 6,
        out_specs=VMEM,
        scratch_shapes=[pltpu.SMEM((slots,), jnp.int32)],
        compiler_params=params(),
        cost_estimate=cost(3 * slots * unit_flops, 3 * slots * tile_bytes),
    )(far_meta, far_queries, far_grads, back, key_tiles, value_tiles, mask)
    back_terms = seq_exchange(far_terms)

    tile_shape = (blocks, BLOCK, cols)
    own_terms, grad_keys, grad_values = pl.pallas_call(
        functools.partial(key_value_kernel, per),
        out_shape=(
            jax.ShapeDtypeStruct(tile_shape, F32),
            jax.ShapeDtypeStruct(tile_shape, BF16),
            jax.ShapeDtypeStruct(tile_shape, BF16),
        ),
        in_specs=[SMEM] + [VMEM] * 9,
        out_specs=(VMEM,) * 3,
        scratch_shapes=[
            pltpu.SMEM((slots,), jnp.int32),
            pltpu.VMEM(tile_shape, F32),
            pltpu.VMEM(tile_shape, F32),
        ],
        compiler_params=params(),
        cost_estimate=cost(5 * slots * unit_flops, 3 * slots * tile_bytes),
    )(far_meta, far_queries, far_grads, back, query_tiles, grad_tiles, row_stats_all, key_tiles, value_tiles, mask)

    contract_rows = (((0,), (0,)), ((), ()))
    contract_cols = (((1,), (1,)), ((), ()))
    grad_key_value = jnp.concatenate(
        [grad_keys.reshape(nodes, cols), grad_values.reshape(nodes, cols)], axis=1
    )
    term_key_value = lax.dot_general(gathered, grad_key_value, contract_rows, preferred_element_type=F32)
    rows = head_exchange(grad_key_value).reshape(-1, n_head, 2, cols)
    rows_key = rows[:, :, 0].reshape(-1, n_head * cols)
    rows_value = rows[:, :, 1].reshape(-1, n_head * cols)
    summed = lax.dot_general(rows_key, w_all[1], contract_cols, preferred_element_type=F32)
    summed = summed + lax.dot_general(rows_value, w_all[2], contract_cols, preferred_element_type=F32)

    grad_query = pl.pallas_call(
        query_sum_kernel,
        out_shape=jax.ShapeDtypeStruct(tile_shape, BF16),
        in_specs=[SMEM, SMEM, VMEM, VMEM],
        out_specs=VMEM,
        compiler_params=params(),
        cost_estimate=cost(0, slots * tile_bytes),
    )(slot_of, counts, own_terms, back_terms).reshape(nodes, cols)
    term_query = lax.dot_general(gathered, grad_query, contract_rows, preferred_element_type=F32)
    weight_terms = jnp.concatenate([term_query, term_key_value], axis=1).astype(BF16)
    weight_terms = seq_exchange(weight_terms.reshape(n_seq, -1, 3 * cols))
    weight_grads = jnp.sum(weight_terms.astype(F32), axis=0)
    rows_query = head_exchange(grad_query)
    summed = summed + lax.dot_general(rows_query, w_all[0], contract_cols, preferred_element_type=F32)
    return (
        summed.astype(BF16),
        weight_grads[:, :cols],
        weight_grads[:, cols : 2 * cols],
        weight_grads[:, 2 * cols :],
    )


def solution(mesh):
    placed = (
        P(("seq", "head"), None),
        P(None, "head"),
        P(None, "head"),
        P(None, "head"),
        P(("seq", "head"), None),
        P("seq", None),
        P("seq"),
    )
    return jax.shard_map(
        shards,
        mesh=mesh,
        in_specs=placed,
        out_specs=(P(("seq", "head"), None), P("seq", "head"), P("seq", "head"), P("seq", "head")),
        check_vma=False,
    )
```

```python
import functools

import jax
import jax.numpy as jnp
from jax import lax
from jax.experimental import pallas as pl
from jax.experimental.pallas import tpu as pltpu
from jax.sharding import PartitionSpec as P

HDIM = 64
BLOCK = 128
KB = 4
BF16 = jnp.bfloat16
F32 = jnp.float32
SCALE = HDIM ** (-0.5)
GROUP = 6
VMEM_LIMIT = 56 * 1024 * 1024
VMEM = pl.BlockSpec(memory_space=pltpu.VMEM)
SMEM = pl.BlockSpec(memory_space=pltpu.SMEM)
NT = (((1,), (1,)), ((), ()))
TN = (((0,), (0,)), ((), ()))


def params():
    return pltpu.CompilerParams(vmem_limit_bytes=VMEM_LIMIT)


def cost(flops, moved):
    return pl.CostEstimate(flops=int(flops), bytes_accessed=int(moved), transcendentals=0)


def head_mask(width, scale):
    heads = width // HDIM
    row_head = jnp.arange(heads * BLOCK)[:, None] // BLOCK
    col_head = jnp.arange(width)[None, :] // HDIM
    return jnp.where(row_head == col_head, scale, 0.0).astype(BF16)


def by_head(tile, mask_ref):
    heads = mask_ref.shape[0] // BLOCK
    return jnp.concatenate([tile] * heads, axis=0) * mask_ref[...]


def products(key_heads, value_heads, query, grad):
    heads = key_heads.shape[0] // BLOCK
    scores = lax.dot_general(key_heads, query, NT, preferred_element_type=F32)
    grad_probs = lax.dot_general(value_heads, grad, NT, preferred_element_type=F32)
    return scores.reshape(heads, BLOCK, BLOCK), grad_probs.reshape(heads, BLOCK, BLOCK)


def row_stats(scores, grad_probs):
    top = jnp.max(scores, axis=1, keepdims=True)
    unnorm = jnp.exp(scores - top)
    total = jnp.sum(unnorm, axis=1)
    weighted = jnp.sum(unnorm * grad_probs, axis=1)
    return top[:, 0] + jnp.log(total), weighted / total


def entry_grads(scores, grad_probs, stats):
    heads = scores.shape[0]
    probs = jnp.exp(scores - stats[:heads][:, None, :])
    grad_scores = probs * (grad_probs - stats[heads:][:, None, :])
    flat = (heads * BLOCK, BLOCK)
    return probs.astype(BF16).reshape(flat), grad_scores.astype(BF16).reshape(flat)


def group_of(blocks):
    return GROUP if blocks % GROUP == 0 else 1


def slot_rows(ref, slot, per):
    return ref[slot // per, pl.ds(lax.rem(slot, per) * BLOCK, BLOCK), :]


def remote_stats_kernel(
    per,
    count_ref,
    order_ref,
    meta_ref,
    query_ref,
    grad_ref,
    key_ref,
    value_ref,
    key_mask_ref,
    mask_ref,
    out_ref,
):
    heads = mask_ref.shape[0] // BLOCK
    out_ref[...] = jnp.zeros_like(out_ref)
    n = count_ref[0]

    def step(g, carry):
        picked = [order_ref[jnp.minimum(g * GROUP + u, n - 1)] for u in range(GROUP)]
        pairs = [
            products(
                by_head(key_ref[meta_ref[slot]], key_mask_ref),
                by_head(value_ref[meta_ref[slot]], mask_ref),
                slot_rows(query_ref, slot, per),
                slot_rows(grad_ref, slot, per),
            )
            for slot in picked
        ]
        for slot, pair in zip(picked, pairs):
            lse, delta = row_stats(*pair)
            out_ref[slot, 0:heads] = lse
            out_ref[slot, heads : 2 * heads] = delta
        return carry

    lax.fori_loop(0, pl.cdiv(n, GROUP), step, 0)


def own_stats_kernel(query_ref, grad_ref, key_ref, value_ref, key_mask_ref, mask_ref, out_ref):
    heads = mask_ref.shape[0] // BLOCK
    blocks = query_ref.shape[0]
    group = group_of(blocks)

    def step(g, carry):
        picked = [g * group + u for u in range(group)]
        pairs = [
            products(
                by_head(key_ref[b], key_mask_ref),
                by_head(value_ref[b], mask_ref),
                query_ref[b],
                grad_ref[b],
            )
            for b in picked
        ]
        for b, pair in zip(picked, pairs):
            lse, delta = row_stats(*pair)
            out_ref[b, 0:heads] = lse
            out_ref[b, heads : 2 * heads] = delta
        return carry

    lax.fori_loop(0, blocks // group, step, 0)


def merge_kernel(slot_ref, count_ref, own_ref, far_ref, row_ref, back_ref, lse_ref, delta_ref):
    blocks = own_ref.shape[0]
    heads = own_ref.shape[1] // 2
    back_ref[...] = jnp.zeros_like(back_ref)
    for b in range(blocks):
        for j in range(KB - 1):
            live = count_ref[b] > j + 1
            stats = far_ref[slot_ref[b * (KB - 1) + j]]
            lse_ref[j, b] = jnp.where(live, stats[:heads], -1e30)
            delta_ref[j, b] = jnp.where(live, stats[heads:], 0.0)
    own = own_ref[...]
    lses = [own[:, :heads]] + [lse_ref[j] for j in range(KB - 1)]
    deltas = [own[:, heads:]] + [delta_ref[j] for j in range(KB - 1)]
    top = functools.reduce(jnp.maximum, lses)
    weights = [jnp.exp(v - top) for v in lses]
    total = sum(weights)
    row_ref[:, :heads] = top + jnp.log(total)
    row_ref[:, heads:] = sum(w * d for w, d in zip(weights, deltas)) / total
    for b in range(blocks):
        for j in range(KB - 1):
            back_ref[slot_ref[b * (KB - 1) + j]] = row_ref[b]


def pick_heads(stacked):
    width = stacked.shape[1]
    heads = width // HDIM
    col_head = lax.broadcasted_iota(jnp.int32, (BLOCK, width), 1) // HDIM
    picked = stacked[:BLOCK]
    for h in range(1, heads):
        picked = jnp.where(col_head == h, stacked[h * BLOCK : (h + 1) * BLOCK], picked)
    return picked


def across_heads(tile, mask_ref):
    heads = mask_ref.shape[1] // BLOCK
    return jnp.concatenate([tile] * heads, axis=1) * mask_ref[...]


def far_query_kernel(
    per,
    count_ref,
    order_ref,
    meta_ref,
    query_ref,
    grad_ref,
    stats_ref,
    key_ref,
    value_ref,
    key_across_ref,
    key_mask_ref,
    mask_ref,
    across_mask_ref,
    out_ref,
):
    n = count_ref[0]

    def step(g, carry):
        picked = [order_ref[jnp.minimum(g * GROUP + u, n - 1)] for u in range(GROUP)]
        pairs = [
            products(
                by_head(key_ref[meta_ref[slot]], key_mask_ref),
                by_head(value_ref[meta_ref[slot]], mask_ref),
                slot_rows(query_ref, slot, per),
                slot_rows(grad_ref, slot, per),
            )
            for slot in picked
        ]
        grads = [entry_grads(*pair, stats_ref[slot])[1] for slot, pair in zip(picked, pairs)]
        for slot, grad_scores in zip(picked, grads):
            key_across = across_heads(key_across_ref[meta_ref[slot]], across_mask_ref)
            term = jnp.dot(key_across, grad_scores, preferred_element_type=F32)
            out_ref[slot] = term.astype(BF16)
        return carry

    lax.fori_loop(0, pl.cdiv(n, GROUP), step, 0)


def key_value_kernel(
    per,
    target_ref,
    count_ref,
    order_ref,
    meta_ref,
    far_query_ref,
    far_grad_ref,
    far_stats_ref,
    query_ref,
    grad_ref,
    stats_ref,
    key_ref,
    value_ref,
    key_across_ref,
    key_mask_ref,
    mask_ref,
    across_mask_ref,
    own_term_ref,
    out_ref,
    *rest,
):
    chunk_refs, (key_sum, value_sum) = rest[:-2], rest[-2:]
    blocks = query_ref.shape[0]
    width = query_ref.shape[2]
    group = group_of(blocks)

    def own(g, carry):
        picked = [g * group + u for u in range(group)]
        pairs = [
            products(
                by_head(key_ref[b], key_mask_ref),
                by_head(value_ref[b], mask_ref),
                query_ref[b],
                grad_ref[b],
            )
            for b in picked
        ]
        grads = [entry_grads(*pair, stats_ref[b]) for b, pair in zip(picked, pairs)]
        for b, (probs, grad_scores) in zip(picked, grads):
            key_across = across_heads(key_across_ref[b], across_mask_ref)
            own_term_ref[b] = jnp.dot(key_across, grad_scores, preferred_element_type=F32)
            key_sum[b] = pick_heads(jnp.dot(grad_scores, query_ref[b], preferred_element_type=F32))
            value_sum[b] = pick_heads(jnp.dot(probs, grad_ref[b], preferred_element_type=F32))
        return carry

    lax.fori_loop(0, blocks // group, own, 0)
    n = count_ref[0]

    def far(g, carry):
        places = [g * GROUP + u for u in range(GROUP)]
        picked = [order_ref[jnp.minimum(at, n - 1)] for at in places]
        tiles = [
            (slot_rows(far_query_ref, slot, per), slot_rows(far_grad_ref, slot, per)) for slot in picked
        ]
        pairs = [
            products(
                by_head(key_ref[meta_ref[slot]], key_mask_ref),
                by_head(value_ref[meta_ref[slot]], mask_ref),
                *tile,
            )
            for slot, tile in zip(picked, tiles)
        ]
        grads = [entry_grads(*pair, far_stats_ref[slot]) for slot, pair in zip(picked, pairs)]
        terms = [
            (
                pick_heads(jnp.dot(grad_scores, query, preferred_element_type=F32)),
                pick_heads(jnp.dot(probs, grad, preferred_element_type=F32)),
            )
            for (probs, grad_scores), (query, grad) in zip(grads, tiles)
        ]
        for at, slot, (key_term, value_term) in zip(places, picked, terms):
            block = meta_ref[slot]
            key_sum[block] += jnp.where(at < n, key_term, 0.0)
            value_sum[block] += jnp.where(at < n, value_term, 0.0)
        return carry

    lax.fori_loop(0, pl.cdiv(n, GROUP), far, 0)
    for b in range(blocks):
        rows = slice(b * BLOCK, (b + 1) * BLOCK)
        out_ref[rows, :width] = (key_sum[b] * SCALE).astype(BF16)
        out_ref[rows, width:] = value_sum[b].astype(BF16)
    copy_chunks(target_ref, out_ref, chunk_refs)


def copy_chunks(target_ref, out_ref, chunk_refs):
    for i, chunk_ref in enumerate(chunk_refs):
        rows = chunk_ref.shape[0]
        chunk_ref[...] = out_ref[pl.ds(pl.multiple_of(target_ref[i] * rows, BLOCK), rows), :]


def query_sum_kernel(target_ref, slot_ref, count_ref, own_ref, far_ref, out_ref, *chunk_refs):
    blocks = own_ref.shape[0]

    for b in range(blocks):
        total = own_ref[b]
        for j in range(KB - 1):
            term = far_ref[slot_ref[b * (KB - 1) + j]].astype(F32)
            total = total + jnp.where(count_ref[b] > j + 1, term, 0.0)
        out_ref[b * BLOCK : (b + 1) * BLOCK, :] = total.T.astype(BF16)
    copy_chunks(target_ref, out_ref, chunk_refs)


def rows_kernel(halves, first, width, *refs):
    n = len(halves)
    chunks = jnp.concatenate([ref[...] for ref in refs[:n]], axis=1)
    weight_refs = list(refs[n : n + sum(halves)])
    start_ref, out_ref = refs[-2:]
    depth = out_ref.shape[1] // 2
    sides = ([], [])
    for count in halves:
        pieces = [weight_refs.pop(0) for _ in range(count)]
        for half in range(2):
            if count == 2:
                sides[half].append(pieces[half][:, first : first + width])
            else:
                sides[half].append(pieces[0][half * depth : (half + 1) * depth, first : first + width])
    for half in range(2):
        columns = slice(half * depth, (half + 1) * depth)
        total = lax.dot_general(
            chunks, jnp.concatenate(sides[half], axis=1), NT, preferred_element_type=F32
        )
        if start_ref is not None:
            total = total + start_ref[:, columns]
        out_ref[:, columns] = total.astype(out_ref.dtype)


def first_rows_kernel(halves, first, width, *refs):
    rows_kernel(halves, first, width, *refs[:-1], None, refs[-1])


def project_kernel(places, source_ref, *refs):
    n = len(places)
    weight_ref, query_ref, key_ref, value_ref, out_ref = refs[n:]
    cols = query_ref.shape[1]
    for i, (index, half) in enumerate(places):
        rows = refs[i].shape[0]
        start = source_ref[index] * (rows if half is None else 2 * rows) + (half or 0) * rows
        span = pl.ds(pl.multiple_of(start, 64), rows)
        out_ref[span, :] = refs[i][...]
        result = jnp.dot(refs[i][...], weight_ref[...], preferred_element_type=F32)
        for j, ref in enumerate((query_ref, key_ref, value_ref)):
            ref[span, :] = result[:, j * cols : (j + 1) * cols].astype(BF16)


def pack_kernel(per, peers_step, source_ref, tile_ref, *rest):
    out_ref = rest[-1]
    first = pl.program_id(0) * peers_step
    for p in range(peers_step):
        for r in range(per):
            out_ref[p, r * BLOCK : (r + 1) * BLOCK, :] = tile_ref[source_ref[(first + p) * per + r]]
    if len(rest) == 2:
        out_ref[:, per * BLOCK :, :] = rest[0][...]


def pack(tiles, source, meta, n_seq, per):
    blocks, _, cols = tiles.shape
    peers_step = 4 if n_seq % 4 == 0 else 1
    extra = 0 if meta is None else meta.shape[1]
    rows = per * BLOCK + extra
    in_specs = [pl.BlockSpec((blocks, BLOCK, cols), lambda i, s: (0, 0, 0))]
    operands = [tiles]
    if meta is not None:
        in_specs.append(pl.BlockSpec((peers_step, extra, cols), lambda i, s: (i, 0, 0)))
        operands.append(meta)
    return pl.pallas_call(
        functools.partial(pack_kernel, per, peers_step),
        grid_spec=pltpu.PrefetchScalarGridSpec(
            num_scalar_prefetch=1,
            grid=(n_seq // peers_step,),
            in_specs=in_specs,
            out_specs=pl.BlockSpec((peers_step, rows, cols), lambda i, s: (i, 0, 0)),
        ),
        out_shape=jax.ShapeDtypeStruct((n_seq, rows, cols), BF16),
        compiler_params=params(),
        cost_estimate=cost(0, 2 * 2 * n_seq * rows * cols),
    )(source, *operands)


def seq_exchange(x):
    return lax.all_to_all(x, "seq", split_axis=0, concat_axis=0, tiled=True)


def head_pairs(step, swap):
    n_head = lax.axis_size("head")
    return [(h, (h + 2 * step) % n_head ^ swap) for h in range(n_head)]


def places_from(n_head):
    return [(step, swap) for step in range(n_head // 2) for swap in range(2)]


def head_gather(x):
    n_head = lax.axis_size("head")
    rounds = n_head // 2
    half = x.shape[0] // 2
    found = {0: [x]}
    up = down = x
    for step in range(1, rounds // 2 + 1):
        if 2 * step < rounds:
            up = lax.ppermute(up, "head", head_pairs(1, 0))
            down = lax.ppermute(down, "head", head_pairs(-1, 0))
            found[step], found[rounds - step] = [up], [down]
        else:
            found[step] = [
                lax.ppermute(up[:half], "head", head_pairs(1, 0)),
                lax.ppermute(down[half:], "head", head_pairs(-1, 0)),
            ]
    pieces = {}
    for step, blocks in found.items():
        pieces[step, 0] = blocks
        pieces[step, 1] = [lax.ppermute(b, "head", head_pairs(0, 1)) for b in blocks]
    return pieces


def head_send(chunks):
    order = places_from(lax.axis_size("head"))
    return [
        c if place == (0, 0) else lax.ppermute(c, "head", head_pairs(*place))
        for place, c in zip(order, chunks)
    ]


def shards(node_input, w_query, w_key, w_value, grad_context, key_blocks, counts):
    n_seq = lax.axis_size("seq")
    n_head = lax.axis_size("head")
    me = lax.axis_index("head")
    cols = w_query.shape[1]
    heads = cols // HDIM
    blocks = key_blocks.shape[0]
    nodes = blocks * BLOCK
    per = max(2, 3 * blocks * (KB - 1) // (2 * n_seq) + 1)
    slots = n_seq * per
    key_mask = head_mask(cols, SCALE)
    mask = head_mask(cols, 1.0)
    order = places_from(n_head)
    steps = jnp.array([p[0] for p in order], jnp.int32)
    swaps = jnp.array([p[1] for p in order], jnp.int32)
    targets = (lax.rem(me // 2 + steps, n_head // 2) * 2) + (lax.rem(me, 2) + swaps) % 2
    sources = (lax.rem(me // 2 - steps + n_head // 2, n_head // 2) * 2) + (lax.rem(me, 2) + swaps) % 2

    remote = key_blocks[:, 1:].reshape(-1)
    entries = remote.shape[0]
    owner = remote // blocks
    inner = remote % blocks
    numbers = jnp.arange(entries, dtype=jnp.int32)
    live = (numbers % (KB - 1)) + 1 < counts[numbers // (KB - 1)]
    before = (owner[:, None] == owner[None, :]) & (numbers[None, :] < numbers[:, None])
    slot_of = owner * per + jnp.sum(before.astype(jnp.int32), axis=1)
    taken = slot_of[None, :] == jnp.arange(slots, dtype=jnp.int32)[:, None]
    source = jnp.sum(jnp.where(taken, numbers[None, :] // (KB - 1), 0), axis=1)
    asked = jnp.sum(jnp.where(taken & live[None, :], inner[None, :] + 1, 0), axis=1) - 1
    meta = jnp.broadcast_to(
        jnp.pad(asked.reshape(n_seq, per), ((0, 0), (0, 16 - per)))[:, :, None], (n_seq, 16, cols)
    ).astype(BF16)

    upstream = lax.all_to_all(grad_context, "head", split_axis=1, concat_axis=0, tiled=True)
    grad_tiles = upstream.reshape(blocks, BLOCK, cols)
    far_grads = seq_exchange(pack(grad_tiles, source, meta, n_seq, per))
    far_meta = far_grads[:, per * BLOCK : per * BLOCK + per, 0].astype(jnp.int32).reshape(-1)
    slot_numbers = jnp.arange(slots, dtype=jnp.int32)
    wanted = far_meta >= 0
    ahead = wanted[None, :] & (slot_numbers[None, :] < slot_numbers[:, None])
    rank = jnp.where(wanted, jnp.sum(ahead.astype(jnp.int32), axis=1), slots)
    far_order = jnp.sum(
        jnp.where(rank[None, :] == slot_numbers[:, None], slot_numbers[None, :], 0), axis=1
    )
    far_count = jnp.sum(wanted.astype(jnp.int32)).reshape(1)
    far_list = (far_count, far_order, far_meta)

    found = head_gather(node_input)
    places, pieces = [], []
    for i, place in enumerate(order):
        for half, piece in enumerate(found[place]):
            places.append((i, None if len(found[place]) == 1 else half))
            pieces.append(piece)
    w_all = jnp.concatenate([w_query, w_key, w_value], axis=1)
    queries, keys, values, gathered = pl.pallas_call(
        functools.partial(project_kernel, places),
        out_shape=(jax.ShapeDtypeStruct((nodes, cols), BF16),) * 3
        + (jax.ShapeDtypeStruct((nodes, node_input.shape[1]), BF16),),
        in_specs=[SMEM] + [VMEM] * (len(pieces) + 1),
        out_specs=(VMEM,) * 4,
        compiler_params=params(),
        cost_estimate=cost(6 * nodes * node_input.shape[1] * cols, 4 * nodes * node_input.shape[1]),
    )(sources, *pieces, w_all)
    query_tiles = queries.reshape(blocks, BLOCK, cols)
    far_queries = seq_exchange(pack(query_tiles, source, None, n_seq, per))
    key_tiles = keys.reshape(blocks, BLOCK, cols)
    value_tiles = values.reshape(blocks, BLOCK, cols)

    w_all, _ = lax.optimization_barrier((w_all, queries))
    found = head_gather(w_all)
    halves = [len(found[place]) for place in order]
    w_pieces = [piece for place in order for piece in found[place]]
    far_queries, *w_pieces = lax.optimization_barrier((far_queries, *w_pieces))
    key_across = keys.reshape(blocks, BLOCK, cols).transpose(0, 2, 1)
    across_mask = key_mask.T

    unit_flops = 2 * heads * BLOCK * BLOCK * cols
    tile_bytes = 2 * BLOCK * cols
    stats_shape = jax.ShapeDtypeStruct((slots, 2 * heads, BLOCK), F32)
    own_stats = pl.pallas_call(
        own_stats_kernel,
        out_shape=jax.ShapeDtypeStruct((blocks, 2 * heads, BLOCK), F32),
        in_specs=[VMEM] * 6,
        out_specs=VMEM,
        compiler_params=params(),
        cost_estimate=cost(2 * blocks * unit_flops, 4 * blocks * tile_bytes),
    )(query_tiles, grad_tiles, key_tiles, value_tiles, key_mask, mask)
    far_stats = pl.pallas_call(
        functools.partial(remote_stats_kernel, per),
        out_shape=stats_shape,
        in_specs=[SMEM] * 3 + [VMEM] * 6,
        out_specs=VMEM,
        compiler_params=params(),
        cost_estimate=cost(2 * slots * unit_flops, 2 * slots * tile_bytes),
    )(*far_list, far_queries, far_grads, key_tiles, value_tiles, key_mask, mask)
    row_stats_all, back = pl.pallas_call(
        merge_kernel,
        out_shape=(jax.ShapeDtypeStruct((blocks, 2 * heads, BLOCK), F32), stats_shape),
        in_specs=[SMEM, SMEM, VMEM, VMEM],
        out_specs=(VMEM, VMEM),
        scratch_shapes=[pltpu.VMEM((KB - 1, blocks, heads, BLOCK), F32)] * 2,
        compiler_params=params(),
        cost_estimate=cost(0, 2 * 2 * slots * 4 * heads * BLOCK),
    )(slot_of, counts, own_stats, seq_exchange(far_stats))
    back = seq_exchange(back)

    far_terms = pl.pallas_call(
        functools.partial(far_query_kernel, per),
        out_shape=jax.ShapeDtypeStruct((slots, cols, BLOCK), BF16),
        in_specs=[SMEM] * 3 + [VMEM] * 9,
        out_specs=VMEM,
        compiler_params=params(),
        cost_estimate=cost(3 * slots * unit_flops, 3 * slots * tile_bytes),
    )(
        *far_list,
        far_queries,
        far_grads,
        back,
        key_tiles,
        value_tiles,
        key_across,
        key_mask,
        mask,
        across_mask,
    )
    back_terms = seq_exchange(far_terms)

    rows = nodes // n_head
    tile_shape = (blocks, BLOCK, cols)
    own_terms, grad_key_value, *chunks = pl.pallas_call(
        functools.partial(key_value_kernel, per),
        out_shape=(
            jax.ShapeDtypeStruct((blocks, cols, BLOCK), F32),
            jax.ShapeDtypeStruct((nodes, 2 * cols), BF16),
        )
        + (jax.ShapeDtypeStruct((rows, 2 * cols), BF16),) * n_head,
        in_specs=[SMEM] * 4 + [VMEM] * 12,
        out_specs=(VMEM,) * (2 + n_head),
        scratch_shapes=[
            pltpu.VMEM(tile_shape, F32),
            pltpu.VMEM(tile_shape, F32),
        ],
        compiler_params=params(),
        cost_estimate=cost(5 * slots * unit_flops, 3 * slots * tile_bytes),
    )(
        targets,
        *far_list,
        far_queries,
        far_grads,
        back,
        query_tiles,
        grad_tiles,
        row_stats_all,
        key_tiles,
        value_tiles,
        key_across,
        key_mask,
        mask,
        across_mask,
    )

    contract_rows = (((0,), (0,)), ((), ()))
    chunks = head_send(chunks)
    term_key_value = lax.dot_general(gathered, grad_key_value, contract_rows, preferred_element_type=F32)
    width = w_query.shape[0]
    summed = pl.pallas_call(
        functools.partial(first_rows_kernel, halves, cols, 2 * cols),
        out_shape=jax.ShapeDtypeStruct((rows, width), F32),
        in_specs=[VMEM] * (len(chunks) + len(w_pieces)),
        out_specs=VMEM,
        compiler_params=params(),
        cost_estimate=cost(2 * rows * width * 2 * cols * n_head, 2 * width * 3 * cols * n_head),
    )(*chunks, *w_pieces)

    back_terms, summed = lax.optimization_barrier((back_terms, summed))
    grad_query, *chunks = pl.pallas_call(
        query_sum_kernel,
        out_shape=(jax.ShapeDtypeStruct((nodes, cols), BF16),)
        + (jax.ShapeDtypeStruct((rows, cols), BF16),) * n_head,
        in_specs=[SMEM] * 3 + [VMEM] * 2,
        out_specs=(VMEM,) * (1 + n_head),
        compiler_params=params(),
        cost_estimate=cost(0, slots * tile_bytes),
    )(targets, slot_of, counts, own_terms, back_terms)
    term_query = lax.dot_general(gathered, grad_query, contract_rows, preferred_element_type=F32)
    weight_terms = jnp.concatenate([term_query, term_key_value], axis=1).astype(BF16)
    weight_terms = seq_exchange(weight_terms.reshape(n_seq, -1, 3 * cols))
    weight_grads = jnp.sum(weight_terms.astype(F32), axis=0)
    chunks = head_send(chunks)
    grad_input = pl.pallas_call(
        functools.partial(rows_kernel, halves, 0, cols),
        grid=(1,),
        out_shape=jax.ShapeDtypeStruct((rows, width), BF16),
        in_specs=[VMEM] * n_head
        + [pl.BlockSpec((p.shape[0], cols), lambda i: (0, 0)) for p in w_pieces]
        + [VMEM],
        out_specs=VMEM,
        compiler_params=params(),
        cost_estimate=cost(2 * rows * width * cols * n_head, 2 * width * cols * n_head),
    )(*chunks, *w_pieces, summed)
    return (
        grad_input,
        weight_grads[:, :cols],
        weight_grads[:, cols : 2 * cols],
        weight_grads[:, 2 * cols :],
    )


def solution(mesh):
    placed = (
        P(("seq", "head"), None),
        P(None, "head"),
        P(None, "head"),
        P(None, "head"),
        P(("seq", "head"), None),
        P("seq", None),
        P("seq"),
    )
    return jax.shard_map(
        shards,
        mesh=mesh,
        in_specs=placed,
        out_specs=(P(("seq", "head"), None), P("seq", "head"), P("seq", "head"), P("seq", "head")),
        check_vma=False,
    )
```

```python
import functools

import jax
import jax.numpy as jnp
from jax import lax
from jax.experimental import pallas as pl
from jax.experimental.pallas import tpu as pltpu
from jax.sharding import PartitionSpec as P

HDIM = 64
BLOCK = 128
KB = 4
BF16 = jnp.bfloat16
F32 = jnp.float32
SCALE = HDIM ** (-0.5)
GROUP = 8
MIB = 1024 * 1024
PACK_LIMIT = 8 * MIB
ROWS_LIMIT = 24 * MIB
ATTEND_LIMIT = 28 * MIB
TAIL_LIMIT = 24 * MIB
VMEM = pl.BlockSpec(memory_space=pltpu.VMEM)
SMEM = pl.BlockSpec(memory_space=pltpu.SMEM)
NT = (((1,), (1,)), ((), ()))
TN = (((0,), (0,)), ((), ()))


def params(limit):
    return pltpu.CompilerParams(vmem_limit_bytes=limit)


def cost(flops, moved):
    return pl.CostEstimate(flops=int(flops), bytes_accessed=int(moved), transcendentals=0)


def head_mask(width, scale):
    heads = width // HDIM
    row_head = jnp.arange(heads * BLOCK)[:, None] // BLOCK
    col_head = jnp.arange(width)[None, :] // HDIM
    return jnp.where(row_head == col_head, scale, 0.0).astype(BF16)


def by_head(tile, mask_ref):
    heads = mask_ref.shape[0] // BLOCK
    return jnp.concatenate([tile] * heads, axis=0) * mask_ref[...]


def products(key_heads, value_heads, query, grad):
    heads = key_heads.shape[0] // BLOCK
    scores = lax.dot_general(key_heads, query, NT, preferred_element_type=F32)
    grad_probs = lax.dot_general(value_heads, grad, NT, preferred_element_type=F32)
    return scores.reshape(heads, BLOCK, BLOCK), grad_probs.reshape(heads, BLOCK, BLOCK)


def row_stats(scores, grad_probs):
    top = jnp.max(scores, axis=1, keepdims=True)
    unnorm = jnp.exp(scores - top)
    total = jnp.sum(unnorm, axis=1)
    weighted = jnp.sum(unnorm * grad_probs, axis=1)
    return top[:, 0] + jnp.log(total), weighted / total


def entry_grads(scores, grad_probs, stats):
    heads = scores.shape[0]
    probs = jnp.exp(scores - stats[:heads][:, None, :])
    grad_scores = probs * (grad_probs - stats[heads:][:, None, :])
    flat = (heads * BLOCK, BLOCK)
    return probs.astype(BF16).reshape(flat), grad_scores.astype(BF16).reshape(flat)


def group_of(blocks):
    return GROUP if blocks % GROUP == 0 else 1


def tile_rows(ref, block, part, width):
    return ref[pl.ds(pl.multiple_of(block * BLOCK, BLOCK), BLOCK), part * width : (part + 1) * width]


def slot_rows(ref, slot, per):
    return ref[slot // per, pl.ds(lax.rem(slot, per) * BLOCK, BLOCK), :]


def remote_stats_kernel(
    per,
    count_ref,
    order_ref,
    meta_ref,
    query_ref,
    grad_ref,
    kv_ref,
    key_mask_ref,
    mask_ref,
    out_ref,
):
    heads = mask_ref.shape[0] // BLOCK
    width = mask_ref.shape[1]
    out_ref[...] = jnp.zeros_like(out_ref)
    n = count_ref[0]

    def step(g, carry):
        picked = [order_ref[jnp.minimum(g * GROUP + u, n - 1)] for u in range(GROUP)]
        pairs = [
            products(
                by_head(tile_rows(kv_ref, meta_ref[slot], 0, width), key_mask_ref),
                by_head(tile_rows(kv_ref, meta_ref[slot], 1, width), mask_ref),
                slot_rows(query_ref, slot, per),
                slot_rows(grad_ref, slot, per),
            )
            for slot in picked
        ]
        for slot, pair in zip(picked, pairs):
            lse, delta = row_stats(*pair)
            out_ref[slot, 0:heads] = lse
            out_ref[slot, heads : 2 * heads] = delta
        return carry

    lax.fori_loop(0, pl.cdiv(n, GROUP), step, 0)


def own_stats_kernel(query_ref, grad_ref, kv_ref, key_mask_ref, mask_ref, out_ref):
    heads = mask_ref.shape[0] // BLOCK
    width = mask_ref.shape[1]
    blocks = query_ref.shape[0]
    group = group_of(blocks)

    def step(g, carry):
        picked = [g * group + u for u in range(group)]
        pairs = [
            products(
                by_head(tile_rows(kv_ref, b, 0, width), key_mask_ref),
                by_head(tile_rows(kv_ref, b, 1, width), mask_ref),
                query_ref[b],
                grad_ref[b],
            )
            for b in picked
        ]
        for b, pair in zip(picked, pairs):
            lse, delta = row_stats(*pair)
            out_ref[b, 0:heads] = lse
            out_ref[b, heads : 2 * heads] = delta
        return carry

    lax.fori_loop(0, blocks // group, step, 0)


def merge_kernel(slot_ref, count_ref, own_ref, far_ref, row_ref, back_ref, lse_ref, delta_ref):
    blocks = own_ref.shape[0]
    heads = own_ref.shape[1] // 2
    back_ref[...] = jnp.zeros_like(back_ref)
    for b in range(blocks):
        for j in range(KB - 1):
            live = count_ref[b] > j + 1
            stats = far_ref[slot_ref[b * (KB - 1) + j]]
            lse_ref[j, b] = jnp.where(live, stats[:heads], -1e30)
            delta_ref[j, b] = jnp.where(live, stats[heads:], 0.0)
    own = own_ref[...]
    lses = [own[:, :heads]] + [lse_ref[j] for j in range(KB - 1)]
    deltas = [own[:, heads:]] + [delta_ref[j] for j in range(KB - 1)]
    top = functools.reduce(jnp.maximum, lses)
    weights = [jnp.exp(v - top) for v in lses]
    total = sum(weights)
    row_ref[:, :heads] = top + jnp.log(total)
    row_ref[:, heads:] = sum(w * d for w, d in zip(weights, deltas)) / total
    for b in range(blocks):
        for j in range(KB - 1):
            back_ref[slot_ref[b * (KB - 1) + j]] = row_ref[b]


def pick_heads(stacked):
    width = stacked.shape[1]
    heads = width // HDIM
    col_head = lax.broadcasted_iota(jnp.int32, (BLOCK, width), 1) // HDIM
    picked = stacked[:BLOCK]
    for h in range(1, heads):
        picked = jnp.where(col_head == h, stacked[h * BLOCK : (h + 1) * BLOCK], picked)
    return picked


def far_query_kernel(
    per,
    count_ref,
    order_ref,
    meta_ref,
    query_ref,
    grad_ref,
    stats_ref,
    kv_ref,
    key_mask_ref,
    mask_ref,
    out_ref,
):
    n = count_ref[0]
    width = mask_ref.shape[1]

    def step(g, carry):
        picked = [order_ref[jnp.minimum(g * GROUP + u, n - 1)] for u in range(GROUP)]
        pairs = [
            products(
                by_head(tile_rows(kv_ref, meta_ref[slot], 0, width), key_mask_ref),
                by_head(tile_rows(kv_ref, meta_ref[slot], 1, width), mask_ref),
                slot_rows(query_ref, slot, per),
                slot_rows(grad_ref, slot, per),
            )
            for slot in picked
        ]
        grads = [entry_grads(*pair, stats_ref[slot])[1] for slot, pair in zip(picked, pairs)]
        for slot, grad_scores in zip(picked, grads):
            key_heads = by_head(tile_rows(kv_ref, meta_ref[slot], 0, width), key_mask_ref)
            term = lax.dot_general(grad_scores, key_heads, TN, preferred_element_type=F32)
            out_ref[slot] = term.astype(BF16)
        return carry

    lax.fori_loop(0, pl.cdiv(n, GROUP), step, 0)


def key_value_kernel(
    per,
    target_ref,
    count_ref,
    order_ref,
    meta_ref,
    far_query_ref,
    far_grad_ref,
    far_stats_ref,
    query_ref,
    grad_ref,
    stats_ref,
    kv_ref,
    key_mask_ref,
    mask_ref,
    own_term_ref,
    out_ref,
    *rest,
):
    chunk_refs, (key_sum, value_sum) = rest[:-2], rest[-2:]
    blocks = query_ref.shape[0]
    width = query_ref.shape[2]
    group = group_of(blocks)

    def own(g, carry):
        picked = [g * group + u for u in range(group)]
        pairs = [
            products(
                by_head(tile_rows(kv_ref, b, 0, width), key_mask_ref),
                by_head(tile_rows(kv_ref, b, 1, width), mask_ref),
                query_ref[b],
                grad_ref[b],
            )
            for b in picked
        ]
        grads = [entry_grads(*pair, stats_ref[b]) for b, pair in zip(picked, pairs)]
        for b, (probs, grad_scores) in zip(picked, grads):
            key_heads = by_head(tile_rows(kv_ref, b, 0, width), key_mask_ref)
            own_term_ref[b] = lax.dot_general(grad_scores, key_heads, TN, preferred_element_type=F32)
            key_sum[b] = pick_heads(jnp.dot(grad_scores, query_ref[b], preferred_element_type=F32))
            value_sum[b] = pick_heads(jnp.dot(probs, grad_ref[b], preferred_element_type=F32))
        return carry

    lax.fori_loop(0, blocks // group, own, 0)
    n = count_ref[0]

    def far(g, carry):
        places = [g * GROUP + u for u in range(GROUP)]
        picked = [order_ref[jnp.minimum(at, n - 1)] for at in places]
        tiles = [
            (slot_rows(far_query_ref, slot, per), slot_rows(far_grad_ref, slot, per)) for slot in picked
        ]
        pairs = [
            products(
                by_head(tile_rows(kv_ref, meta_ref[slot], 0, width), key_mask_ref),
                by_head(tile_rows(kv_ref, meta_ref[slot], 1, width), mask_ref),
                *tile,
            )
            for slot, tile in zip(picked, tiles)
        ]
        grads = [entry_grads(*pair, far_stats_ref[slot]) for slot, pair in zip(picked, pairs)]
        terms = [
            (
                pick_heads(jnp.dot(grad_scores, query, preferred_element_type=F32)),
                pick_heads(jnp.dot(probs, grad, preferred_element_type=F32)),
            )
            for (probs, grad_scores), (query, grad) in zip(grads, tiles)
        ]
        for at, slot, (key_term, value_term) in zip(places, picked, terms):
            block = meta_ref[slot]
            key_sum[block] += jnp.where(at < n, key_term, 0.0)
            value_sum[block] += jnp.where(at < n, value_term, 0.0)
        return carry

    lax.fori_loop(0, pl.cdiv(n, GROUP), far, 0)
    for b in range(blocks):
        rows = slice(b * BLOCK, (b + 1) * BLOCK)
        out_ref[rows, :width] = (key_sum[b] * SCALE).astype(BF16)
        out_ref[rows, width:] = value_sum[b].astype(BF16)
    copy_chunks(target_ref, out_ref, chunk_refs)


def copy_chunks(target_ref, out_ref, chunk_refs):
    for i, chunk_ref in enumerate(chunk_refs):
        rows = chunk_ref.shape[0]
        chunk_ref[...] = out_ref[pl.ds(pl.multiple_of(target_ref[i] * rows, BLOCK), rows), :]


def query_sum_kernel(target_ref, slot_ref, count_ref, own_ref, far_ref, out_ref, *chunk_refs):
    blocks = own_ref.shape[0]

    for b in range(blocks):
        total = own_ref[b]
        for j in range(KB - 1):
            term = far_ref[slot_ref[b * (KB - 1) + j]].astype(F32)
            total = total + jnp.where(count_ref[b] > j + 1, term, 0.0)
        out_ref[b * BLOCK : (b + 1) * BLOCK, :] = total.astype(BF16)
    copy_chunks(target_ref, out_ref, chunk_refs)


def rows_kernel(n, *refs):
    chunks = jnp.concatenate([ref[...] for ref in refs[:n]], axis=1)
    weight_ref, out_ref = refs[n], refs[-1]
    total = lax.dot_general(chunks, weight_ref[...], NT, preferred_element_type=F32)
    if len(refs) == n + 3:
        total = total + refs[n + 1][...]
    out_ref[...] = total.astype(out_ref.dtype)


def weights_kernel(halves, *refs):
    query_ref, kv_ref = refs[-2:]
    piece_refs = list(refs[:-2])
    width = query_ref.shape[1] // len(halves)
    for i, count in enumerate(halves):
        start = 0
        for _ in range(count):
            piece = piece_refs.pop(0)
            rows = slice(start, start + piece.shape[0])
            start += piece.shape[0]
            query_ref[rows, i * width : (i + 1) * width] = piece[:, :width]
            kv_ref[rows, 2 * i * width : 2 * (i + 1) * width] = piece[:, width:]


def spans(places, source_ref, refs):
    for i, (index, half) in enumerate(places):
        rows = refs[i].shape[0]
        start = source_ref[index] * (rows if half is None else 2 * rows) + (half or 0) * rows
        yield refs[i], pl.ds(pl.multiple_of(start, 64), rows)


def query_kernel(places, source_ref, *refs):
    weight_ref, out_ref = refs[len(places) :]
    for ref, span in spans(places, source_ref, refs):
        out_ref[span, :] = jnp.dot(
            ref[...], weight_ref[...], preferred_element_type=F32
        ).astype(BF16)


def project_kernel(places, source_ref, *refs):
    weight_ref, kv_ref, out_ref = refs[len(places) :]
    for ref, span in spans(places, source_ref, refs):
        out_ref[span, :] = ref[...]
        kv_ref[span, :] = jnp.dot(
            ref[...], weight_ref[...], preferred_element_type=F32
        ).astype(BF16)


def pack_kernel(per, peers_step, extra, source_ref, asked_ref, tile_ref, out_ref):
    first = pl.program_id(0) * peers_step
    for p in range(peers_step):
        at = (first + p) * per
        for r in range(per):
            out_ref[p, r * BLOCK : (r + 1) * BLOCK, :] = tile_ref[source_ref[at + r]]
        if extra:
            row = lax.broadcasted_iota(jnp.int32, (extra, out_ref.shape[2]), 0)
            meta = jnp.zeros(row.shape, F32)
            for r in range(per):
                meta = jnp.where(row == r, asked_ref[at + r].astype(F32), meta)
            out_ref[p, per * BLOCK :, :] = meta.astype(BF16)


def pack(tiles, source, asked, n_seq, per, extra):
    blocks, _, cols = tiles.shape
    peers_step = 4 if n_seq % 4 == 0 else 1
    rows = per * BLOCK + extra
    return pl.pallas_call(
        functools.partial(pack_kernel, per, peers_step, extra),
        grid_spec=pltpu.PrefetchScalarGridSpec(
            num_scalar_prefetch=2,
            grid=(n_seq // peers_step,),
            in_specs=[pl.BlockSpec((blocks, BLOCK, cols), lambda i, s, a: (0, 0, 0))],
            out_specs=pl.BlockSpec((peers_step, rows, cols), lambda i, s, a: (i, 0, 0)),
        ),
        out_shape=jax.ShapeDtypeStruct((n_seq, rows, cols), BF16),
        compiler_params=params(PACK_LIMIT),
        cost_estimate=cost(0, 2 * 2 * n_seq * rows * cols),
    )(source, asked, tiles)


def seq_exchange(x):
    return lax.all_to_all(x, "seq", split_axis=0, concat_axis=0, tiled=True)


def head_pairs(step, swap):
    n_head = lax.axis_size("head")
    return [(h, (h + 2 * step) % n_head ^ swap) for h in range(n_head)]


def places_from(n_head):
    return [(step, swap) for step in range(n_head // 2) for swap in range(2)]


def head_gather(x):
    n_head = lax.axis_size("head")
    rounds = n_head // 2
    half = x.shape[0] // 2
    found = {0: [x]}
    up = down = x
    for step in range(1, rounds // 2 + 1):
        if 2 * step < rounds:
            up = lax.ppermute(up, "head", head_pairs(1, 0))
            down = lax.ppermute(down, "head", head_pairs(-1, 0))
            found[step], found[rounds - step] = [up], [down]
        else:
            found[step] = [
                lax.ppermute(up[:half], "head", head_pairs(1, 0)),
                lax.ppermute(down[half:], "head", head_pairs(-1, 0)),
            ]
    pieces = {}
    for step, blocks in found.items():
        pieces[step, 0] = blocks
        pieces[step, 1] = [lax.ppermute(b, "head", head_pairs(0, 1)) for b in blocks]
    return pieces


def head_send(chunks):
    order = places_from(lax.axis_size("head"))
    return [
        c if place == (0, 0) else lax.ppermute(c, "head", head_pairs(*place))
        for place, c in zip(order, chunks)
    ]


def shards(node_input, w_query, w_key, w_value, grad_context, key_blocks, counts):
    n_seq = lax.axis_size("seq")
    n_head = lax.axis_size("head")
    me = lax.axis_index("head")
    cols = w_query.shape[1]
    heads = cols // HDIM
    blocks = key_blocks.shape[0]
    nodes = blocks * BLOCK
    per = max(2, 3 * blocks * (KB - 1) // (2 * n_seq) + 1)
    slots = n_seq * per
    key_mask = head_mask(cols, SCALE)
    mask = head_mask(cols, 1.0)
    order = places_from(n_head)
    steps = jnp.array([p[0] for p in order], jnp.int32)
    swaps = jnp.array([p[1] for p in order], jnp.int32)
    targets = (lax.rem(me // 2 + steps, n_head // 2) * 2) + (lax.rem(me, 2) + swaps) % 2
    sources = (lax.rem(me // 2 - steps + n_head // 2, n_head // 2) * 2) + (lax.rem(me, 2) + swaps) % 2

    remote = key_blocks[:, 1:].reshape(-1)
    entries = remote.shape[0]
    owner = remote // blocks
    inner = remote % blocks
    numbers = jnp.arange(entries, dtype=jnp.int32)
    live = (numbers % (KB - 1)) + 1 < counts[numbers // (KB - 1)]
    before = (owner[:, None] == owner[None, :]) & (numbers[None, :] < numbers[:, None])
    slot_of = owner * per + jnp.sum(before.astype(jnp.int32), axis=1)
    taken = slot_of[None, :] == jnp.arange(slots, dtype=jnp.int32)[:, None]
    source = jnp.sum(jnp.where(taken, numbers[None, :] // (KB - 1), 0), axis=1)
    asked = jnp.sum(jnp.where(taken & live[None, :], inner[None, :] + 1, 0), axis=1) - 1
    upstream = lax.all_to_all(grad_context, "head", split_axis=1, concat_axis=0, tiled=True)
    grad_tiles = upstream.reshape(blocks, BLOCK, cols)
    far_grads = seq_exchange(pack(grad_tiles, source, asked, n_seq, per, 16))
    far_meta = far_grads[:, per * BLOCK : per * BLOCK + per, 0].astype(jnp.int32).reshape(-1)
    slot_numbers = jnp.arange(slots, dtype=jnp.int32)
    wanted = far_meta >= 0
    ahead = wanted[None, :] & (slot_numbers[None, :] < slot_numbers[:, None])
    rank = jnp.where(wanted, jnp.sum(ahead.astype(jnp.int32), axis=1), slots)
    far_order = jnp.sum(
        jnp.where(rank[None, :] == slot_numbers[:, None], slot_numbers[None, :], 0), axis=1
    )
    far_count = jnp.sum(wanted.astype(jnp.int32)).reshape(1)
    far_list = (far_count, far_order, far_meta)

    width = node_input.shape[1]
    found = head_gather(node_input)
    places, pieces = [], []
    for i, place in enumerate(order):
        for half, piece in enumerate(found[place]):
            places.append((i, None if len(found[place]) == 1 else half))
            pieces.append(piece)
    queries = pl.pallas_call(
        functools.partial(query_kernel, places),
        out_shape=jax.ShapeDtypeStruct((nodes, cols), BF16),
        in_specs=[SMEM] + [VMEM] * (len(pieces) + 1),
        out_specs=VMEM,
        compiler_params=params(ROWS_LIMIT),
        cost_estimate=cost(2 * nodes * width * cols, 2 * nodes * width),
    )(sources, *pieces, w_query)
    query_tiles = queries.reshape(blocks, BLOCK, cols)
    packed = pack(query_tiles, source, asked, n_seq, per, 0)
    far_queries = seq_exchange(packed)
    w_kv = jnp.concatenate([w_key, w_value], axis=1)
    packed, *pieces = lax.optimization_barrier((packed, *pieces))
    kv, gathered = pl.pallas_call(
        functools.partial(project_kernel, places),
        out_shape=(
            jax.ShapeDtypeStruct((nodes, 2 * cols), BF16),
            jax.ShapeDtypeStruct((nodes, width), BF16),
        ),
        in_specs=[SMEM] + [VMEM] * (len(pieces) + 1),
        out_specs=(VMEM,) * 2,
        compiler_params=params(ROWS_LIMIT),
        cost_estimate=cost(4 * nodes * width * cols, 4 * nodes * width),
    )(sources, *pieces, w_kv)

    w_all = jnp.concatenate([w_query, w_key, w_value], axis=1)
    w_all, _ = lax.optimization_barrier((w_all, packed))
    found = head_gather(w_all)
    halves = [len(found[place]) for place in order]
    w_pieces = [piece for place in order for piece in found[place]]
    w_rows, w_kv_rows = pl.pallas_call(
        functools.partial(weights_kernel, halves),
        out_shape=(
            jax.ShapeDtypeStruct((width, n_head * cols), BF16),
            jax.ShapeDtypeStruct((width, n_head * 2 * cols), BF16),
        ),
        in_specs=[VMEM] * len(w_pieces),
        out_specs=(VMEM,) * 2,
        compiler_params=params(ROWS_LIMIT),
        cost_estimate=cost(0, 12 * width * n_head * cols),
    )(*w_pieces)
    far_queries, w_rows, w_kv_rows = lax.optimization_barrier((far_queries, w_rows, w_kv_rows))

    unit_flops = 2 * heads * BLOCK * BLOCK * cols
    tile_bytes = 2 * BLOCK * cols
    stats_shape = jax.ShapeDtypeStruct((slots, 2 * heads, BLOCK), F32)
    own_stats = pl.pallas_call(
        own_stats_kernel,
        out_shape=jax.ShapeDtypeStruct((blocks, 2 * heads, BLOCK), F32),
        in_specs=[VMEM] * 5,
        out_specs=VMEM,
        compiler_params=params(ATTEND_LIMIT),
        cost_estimate=cost(2 * blocks * unit_flops, 4 * blocks * tile_bytes),
    )(query_tiles, grad_tiles, kv, key_mask, mask)
    far_stats = pl.pallas_call(
        functools.partial(remote_stats_kernel, per),
        out_shape=stats_shape,
        in_specs=[SMEM] * 3 + [VMEM] * 5,
        out_specs=VMEM,
        compiler_params=params(ATTEND_LIMIT),
        cost_estimate=cost(2 * slots * unit_flops, 2 * slots * tile_bytes),
    )(*far_list, far_queries, far_grads, kv, key_mask, mask)
    row_stats_all, back = pl.pallas_call(
        merge_kernel,
        out_shape=(jax.ShapeDtypeStruct((blocks, 2 * heads, BLOCK), F32), stats_shape),
        in_specs=[SMEM, SMEM, VMEM, VMEM],
        out_specs=(VMEM, VMEM),
        scratch_shapes=[pltpu.VMEM((KB - 1, blocks, heads, BLOCK), F32)] * 2,
        compiler_params=params(ATTEND_LIMIT),
        cost_estimate=cost(0, 2 * 2 * slots * 4 * heads * BLOCK),
    )(slot_of, counts, own_stats, seq_exchange(far_stats))
    back = seq_exchange(back)

    far_terms = pl.pallas_call(
        functools.partial(far_query_kernel, per),
        out_shape=jax.ShapeDtypeStruct((slots, BLOCK, cols), BF16),
        in_specs=[SMEM] * 3 + [VMEM] * 6,
        out_specs=VMEM,
        compiler_params=params(ATTEND_LIMIT),
        cost_estimate=cost(3 * slots * unit_flops, 3 * slots * tile_bytes),
    )(
        *far_list,
        far_queries,
        far_grads,
        back,
        kv,
        key_mask,
        mask,
    )
    back_terms = seq_exchange(far_terms)

    rows = nodes // n_head
    tile_shape = (blocks, BLOCK, cols)
    own_terms, grad_key_value, *chunks = pl.pallas_call(
        functools.partial(key_value_kernel, per),
        out_shape=(
            jax.ShapeDtypeStruct(tile_shape, F32),
            jax.ShapeDtypeStruct((nodes, 2 * cols), BF16),
        )
        + (jax.ShapeDtypeStruct((rows, 2 * cols), BF16),) * n_head,
        in_specs=[SMEM] * 4 + [VMEM] * 9,
        out_specs=(VMEM,) * (2 + n_head),
        scratch_shapes=[
            pltpu.VMEM(tile_shape, F32),
            pltpu.VMEM(tile_shape, F32),
        ],
        compiler_params=params(ATTEND_LIMIT),
        cost_estimate=cost(5 * slots * unit_flops, 3 * slots * tile_bytes),
    )(
        targets,
        *far_list,
        far_queries,
        far_grads,
        back,
        query_tiles,
        grad_tiles,
        row_stats_all,
        kv,
        key_mask,
        mask,
    )

    contract_rows = (((0,), (0,)), ((), ()))
    chunks = head_send(chunks)
    term_key_value = lax.dot_general(gathered, grad_key_value, contract_rows, preferred_element_type=F32)
    back_terms, *chunks = lax.optimization_barrier((back_terms, *chunks))
    summed = pl.pallas_call(
        functools.partial(rows_kernel, n_head),
        out_shape=jax.ShapeDtypeStruct((rows, width), F32),
        in_specs=[VMEM] * (n_head + 1),
        out_specs=VMEM,
        compiler_params=params(TAIL_LIMIT),
        cost_estimate=cost(2 * rows * width * 2 * cols * n_head, 2 * width * 2 * cols * n_head),
    )(*chunks, w_kv_rows)

    grad_query, *chunks = pl.pallas_call(
        query_sum_kernel,
        out_shape=(jax.ShapeDtypeStruct((nodes, cols), BF16),)
        + (jax.ShapeDtypeStruct((rows, cols), BF16),) * n_head,
        in_specs=[SMEM] * 3 + [VMEM] * 2,
        out_specs=(VMEM,) * (1 + n_head),
        compiler_params=params(TAIL_LIMIT),
        cost_estimate=cost(0, slots * tile_bytes),
    )(targets, slot_of, counts, own_terms, back_terms)
    term_query = lax.dot_general(gathered, grad_query, contract_rows, preferred_element_type=F32)
    weight_terms = jnp.concatenate([term_query, term_key_value], axis=1).astype(BF16)
    weight_terms = seq_exchange(weight_terms.reshape(n_seq, width // n_seq, 3 * cols))
    weight_grads = jnp.sum(weight_terms.astype(F32), axis=0)
    chunks = head_send(chunks)
    grad_input = pl.pallas_call(
        functools.partial(rows_kernel, n_head),
        out_shape=jax.ShapeDtypeStruct((rows, width), BF16),
        in_specs=[VMEM] * (n_head + 2),
        out_specs=VMEM,
        compiler_params=params(TAIL_LIMIT),
        cost_estimate=cost(2 * rows * width * cols * n_head, 2 * width * cols * n_head),
    )(*chunks, w_rows, summed)
    return (
        grad_input,
        weight_grads[:, :cols],
        weight_grads[:, cols : 2 * cols],
        weight_grads[:, 2 * cols :],
    )


def solution(mesh):
    placed = (
        P(("seq", "head"), None),
        P(None, "head"),
        P(None, "head"),
        P(None, "head"),
        P(("seq", "head"), None),
        P("seq", None),
        P("seq"),
    )
    return jax.shard_map(
        shards,
        mesh=mesh,
        in_specs=placed,
        out_specs=(P(("seq", "head"), None), P("seq", "head"), P("seq", "head"), P("seq", "head")),
        check_vma=False,
    )
```

```python
import functools

import jax
import jax.numpy as jnp
from jax import lax
from jax.experimental import pallas as pl
from jax.experimental.pallas import tpu as pltpu
from jax.sharding import PartitionSpec as P

HDIM = 64
BLOCK = 128
KB = 4
BF16 = jnp.bfloat16
F32 = jnp.float32
SCALE = HDIM ** (-0.5)
GROUP = 8
MIB = 1024 * 1024
PACK_LIMIT = 8 * MIB
ROWS_LIMIT = 24 * MIB
ATTEND_LIMIT = 28 * MIB
TAIL_LIMIT = 24 * MIB
VMEM = pl.BlockSpec(memory_space=pltpu.VMEM)
SMEM = pl.BlockSpec(memory_space=pltpu.SMEM)
NT = (((1,), (1,)), ((), ()))
TN = (((0,), (0,)), ((), ()))


def params(limit):
    return pltpu.CompilerParams(vmem_limit_bytes=limit)


def cost(flops, moved):
    return pl.CostEstimate(flops=int(flops), bytes_accessed=int(moved), transcendentals=0)


def head_mask(width, scale):
    heads = width // HDIM
    row_head = jnp.arange(heads * BLOCK)[:, None] // BLOCK
    col_head = jnp.arange(width)[None, :] // HDIM
    return jnp.where(row_head == col_head, scale, 0.0).astype(BF16)


def by_head(tile, mask_ref):
    heads = mask_ref.shape[0] // BLOCK
    return jnp.concatenate([tile] * heads, axis=0) * mask_ref[...]


def products(key_heads, value_heads, query, grad):
    heads = key_heads.shape[0] // BLOCK
    scores = lax.dot_general(key_heads, query, NT, preferred_element_type=F32)
    grad_probs = lax.dot_general(value_heads, grad, NT, preferred_element_type=F32)
    return scores.reshape(heads, BLOCK, BLOCK), grad_probs.reshape(heads, BLOCK, BLOCK)


def row_stats(scores, grad_probs):
    top = jnp.max(scores, axis=1, keepdims=True)
    unnorm = jnp.exp(scores - top)
    total = jnp.sum(unnorm, axis=1)
    weighted = jnp.sum(unnorm * grad_probs, axis=1)
    return top[:, 0] + jnp.log(total), weighted / total


def entry_grads(scores, grad_probs, stats):
    heads = scores.shape[0]
    probs = jnp.exp(scores - stats[:heads][:, None, :])
    grad_scores = probs * (grad_probs - stats[heads:][:, None, :])
    flat = (heads * BLOCK, BLOCK)
    return probs.astype(BF16).reshape(flat), grad_scores.astype(BF16).reshape(flat)


def group_of(blocks):
    return GROUP if blocks % GROUP == 0 else 1


def tile_rows(ref, block, part, width):
    return ref[pl.ds(pl.multiple_of(block * BLOCK, BLOCK), BLOCK), part * width : (part + 1) * width]


def slot_rows(ref, slot, per):
    return ref[slot // per, pl.ds(lax.rem(slot, per) * BLOCK, BLOCK), :]


def remote_stats_kernel(
    per,
    count_ref,
    order_ref,
    meta_ref,
    query_ref,
    grad_ref,
    kv_ref,
    key_mask_ref,
    mask_ref,
    out_ref,
):
    heads = mask_ref.shape[0] // BLOCK
    width = mask_ref.shape[1]
    out_ref[...] = jnp.zeros_like(out_ref)
    n = count_ref[0]

    def step(g, carry):
        picked = [order_ref[jnp.minimum(g * GROUP + u, n - 1)] for u in range(GROUP)]
        pairs = [
            products(
                by_head(tile_rows(kv_ref, meta_ref[slot], 0, width), key_mask_ref),
                by_head(tile_rows(kv_ref, meta_ref[slot], 1, width), mask_ref),
                slot_rows(query_ref, slot, per),
                slot_rows(grad_ref, slot, per),
            )
            for slot in picked
        ]
        for slot, pair in zip(picked, pairs):
            lse, delta = row_stats(*pair)
            out_ref[slot, 0:heads] = lse
            out_ref[slot, heads : 2 * heads] = delta
        return carry

    lax.fori_loop(0, pl.cdiv(n, GROUP), step, 0)


def own_stats_kernel(query_ref, grad_ref, kv_ref, key_mask_ref, mask_ref, out_ref):
    heads = mask_ref.shape[0] // BLOCK
    width = mask_ref.shape[1]
    blocks = query_ref.shape[0]
    group = group_of(blocks)

    def step(g, carry):
        picked = [g * group + u for u in range(group)]
        pairs = [
            products(
                by_head(tile_rows(kv_ref, b, 0, width), key_mask_ref),
                by_head(tile_rows(kv_ref, b, 1, width), mask_ref),
                query_ref[b],
                grad_ref[b],
            )
            for b in picked
        ]
        for b, pair in zip(picked, pairs):
            lse, delta = row_stats(*pair)
            out_ref[b, 0:heads] = lse
            out_ref[b, heads : 2 * heads] = delta
        return carry

    lax.fori_loop(0, blocks // group, step, 0)


def merge_kernel(slot_ref, count_ref, own_ref, far_ref, row_ref, back_ref, lse_ref, delta_ref):
    blocks = own_ref.shape[0]
    heads = own_ref.shape[1] // 2
    back_ref[...] = jnp.zeros_like(back_ref)
    for b in range(blocks):
        for j in range(KB - 1):
            live = count_ref[b] > j + 1
            stats = far_ref[slot_ref[b * (KB - 1) + j]]
            lse_ref[j, b] = jnp.where(live, stats[:heads], -1e30)
            delta_ref[j, b] = jnp.where(live, stats[heads:], 0.0)
    own = own_ref[...]
    lses = [own[:, :heads]] + [lse_ref[j] for j in range(KB - 1)]
    deltas = [own[:, heads:]] + [delta_ref[j] for j in range(KB - 1)]
    top = functools.reduce(jnp.maximum, lses)
    weights = [jnp.exp(v - top) for v in lses]
    total = sum(weights)
    row_ref[:, :heads] = top + jnp.log(total)
    row_ref[:, heads:] = sum(w * d for w, d in zip(weights, deltas)) / total
    for b in range(blocks):
        for j in range(KB - 1):
            back_ref[slot_ref[b * (KB - 1) + j]] = row_ref[b]


def pick_heads(stacked):
    width = stacked.shape[1]
    heads = width // HDIM
    col_head = lax.broadcasted_iota(jnp.int32, (BLOCK, width), 1) // HDIM
    picked = stacked[:BLOCK]
    for h in range(1, heads):
        picked = jnp.where(col_head == h, stacked[h * BLOCK : (h + 1) * BLOCK], picked)
    return picked


def far_query_kernel(
    per,
    count_ref,
    order_ref,
    meta_ref,
    query_ref,
    grad_ref,
    stats_ref,
    kv_ref,
    key_mask_ref,
    mask_ref,
    out_ref,
):
    n = count_ref[0]
    width = mask_ref.shape[1]

    def step(g, carry):
        picked = [order_ref[jnp.minimum(g * GROUP + u, n - 1)] for u in range(GROUP)]
        pairs = [
            products(
                by_head(tile_rows(kv_ref, meta_ref[slot], 0, width), key_mask_ref),
                by_head(tile_rows(kv_ref, meta_ref[slot], 1, width), mask_ref),
                slot_rows(query_ref, slot, per),
                slot_rows(grad_ref, slot, per),
            )
            for slot in picked
        ]
        grads = [entry_grads(*pair, stats_ref[slot])[1] for slot, pair in zip(picked, pairs)]
        for slot, grad_scores in zip(picked, grads):
            key_heads = by_head(tile_rows(kv_ref, meta_ref[slot], 0, width), key_mask_ref)
            term = lax.dot_general(grad_scores, key_heads, TN, preferred_element_type=F32)
            out_ref[slot] = term.astype(BF16)
        return carry

    lax.fori_loop(0, pl.cdiv(n, GROUP), step, 0)


def key_value_kernel(
    per,
    target_ref,
    count_ref,
    order_ref,
    meta_ref,
    far_query_ref,
    far_grad_ref,
    far_stats_ref,
    query_ref,
    grad_ref,
    stats_ref,
    kv_ref,
    key_mask_ref,
    mask_ref,
    own_term_ref,
    out_ref,
    *rest,
):
    chunk_refs, (key_sum, value_sum) = rest[:-2], rest[-2:]
    blocks = query_ref.shape[0]
    width = query_ref.shape[2]
    group = group_of(blocks)

    def own(g, carry):
        picked = [g * group + u for u in range(group)]
        pairs = [
            products(
                by_head(tile_rows(kv_ref, b, 0, width), key_mask_ref),
                by_head(tile_rows(kv_ref, b, 1, width), mask_ref),
                query_ref[b],
                grad_ref[b],
            )
            for b in picked
        ]
        grads = [entry_grads(*pair, stats_ref[b]) for b, pair in zip(picked, pairs)]
        for b, (probs, grad_scores) in zip(picked, grads):
            key_heads = by_head(tile_rows(kv_ref, b, 0, width), key_mask_ref)
            own_term_ref[b] = lax.dot_general(grad_scores, key_heads, TN, preferred_element_type=F32)
            key_sum[b] = pick_heads(jnp.dot(grad_scores, query_ref[b], preferred_element_type=F32))
            value_sum[b] = pick_heads(jnp.dot(probs, grad_ref[b], preferred_element_type=F32))
        return carry

    lax.fori_loop(0, blocks // group, own, 0)
    n = count_ref[0]

    def far(g, carry):
        places = [g * GROUP + u for u in range(GROUP)]
        picked = [order_ref[jnp.minimum(at, n - 1)] for at in places]
        tiles = [
            (slot_rows(far_query_ref, slot, per), slot_rows(far_grad_ref, slot, per)) for slot in picked
        ]
        pairs = [
            products(
                by_head(tile_rows(kv_ref, meta_ref[slot], 0, width), key_mask_ref),
                by_head(tile_rows(kv_ref, meta_ref[slot], 1, width), mask_ref),
                *tile,
            )
            for slot, tile in zip(picked, tiles)
        ]
        grads = [entry_grads(*pair, far_stats_ref[slot]) for slot, pair in zip(picked, pairs)]
        terms = [
            (
                pick_heads(jnp.dot(grad_scores, query, preferred_element_type=F32)),
                pick_heads(jnp.dot(probs, grad, preferred_element_type=F32)),
            )
            for (probs, grad_scores), (query, grad) in zip(grads, tiles)
        ]
        for at, slot, (key_term, value_term) in zip(places, picked, terms):
            block = meta_ref[slot]
            key_sum[block] += jnp.where(at < n, key_term, 0.0)
            value_sum[block] += jnp.where(at < n, value_term, 0.0)
        return carry

    lax.fori_loop(0, pl.cdiv(n, GROUP), far, 0)
    for b in range(blocks):
        rows = slice(b * BLOCK, (b + 1) * BLOCK)
        out_ref[rows, :width] = (key_sum[b] * SCALE).astype(BF16)
        out_ref[rows, width:] = value_sum[b].astype(BF16)
    copy_chunks(target_ref, out_ref, chunk_refs)


def copy_chunks(target_ref, out_ref, chunk_refs):
    for i, chunk_ref in enumerate(chunk_refs):
        rows = chunk_ref.shape[0]
        chunk_ref[...] = out_ref[pl.ds(pl.multiple_of(target_ref[i] * rows, BLOCK), rows), :]


def query_sum_kernel(target_ref, slot_ref, count_ref, own_ref, far_ref, out_ref, *chunk_refs):
    blocks = own_ref.shape[0]

    for b in range(blocks):
        total = own_ref[b]
        for j in range(KB - 1):
            term = far_ref[slot_ref[b * (KB - 1) + j]].astype(F32)
            total = total + jnp.where(count_ref[b] > j + 1, term, 0.0)
        out_ref[b * BLOCK : (b + 1) * BLOCK, :] = total.astype(BF16)
    copy_chunks(target_ref, out_ref, chunk_refs)


def rows_kernel(n, *refs):
    chunks = jnp.concatenate([ref[...] for ref in refs[:n]], axis=1)
    weight_ref, out_ref = refs[n], refs[-1]
    total = lax.dot_general(chunks, weight_ref[...], NT, preferred_element_type=F32)
    if len(refs) == n + 3:
        total = total + refs[n + 1][...]
    out_ref[...] = total.astype(out_ref.dtype)


def weights_kernel(halves, *refs):
    query_ref, kv_ref = refs[-2:]
    piece_refs = list(refs[:-2])
    width = query_ref.shape[1] // len(halves)
    for i, count in enumerate(halves):
        start = 0
        for _ in range(count):
            piece = piece_refs.pop(0)
            rows = slice(start, start + piece.shape[0])
            start += piece.shape[0]
            query_ref[rows, i * width : (i + 1) * width] = piece[:, :width]
            kv_ref[rows, 2 * i * width : 2 * (i + 1) * width] = piece[:, width:]


def spans(places, source_ref, refs):
    for i, (index, half) in enumerate(places):
        rows = refs[i].shape[0]
        start = source_ref[index] * (rows if half is None else 2 * rows) + (half or 0) * rows
        yield refs[i], pl.ds(pl.multiple_of(start, 64), rows)


def query_kernel(places, source_ref, *refs):
    weight_ref, out_ref = refs[len(places) :]
    for ref, span in spans(places, source_ref, refs):
        out_ref[span, :] = jnp.dot(
            ref[...], weight_ref[...], preferred_element_type=F32
        ).astype(BF16)


def project_kernel(places, source_ref, *refs):
    weight_ref, kv_ref, out_ref = refs[len(places) :]
    for ref, span in spans(places, source_ref, refs):
        out_ref[span, :] = ref[...]
        kv_ref[span, :] = jnp.dot(
            ref[...], weight_ref[...], preferred_element_type=F32
        ).astype(BF16)


def pack_kernel(per, peers_step, extra, source_ref, asked_ref, tile_ref, out_ref):
    first = pl.program_id(0) * peers_step
    for p in range(peers_step):
        at = (first + p) * per
        for r in range(per):
            out_ref[p, r * BLOCK : (r + 1) * BLOCK, :] = tile_ref[source_ref[at + r]]
        if extra:
            row = lax.broadcasted_iota(jnp.int32, (extra, out_ref.shape[2]), 0)
            meta = jnp.zeros(row.shape, F32)
            for r in range(per):
                meta = jnp.where(row == r, asked_ref[at + r].astype(F32), meta)
            out_ref[p, per * BLOCK :, :] = meta.astype(BF16)


def pack(tiles, source, asked, n_seq, per, extra):
    blocks, _, cols = tiles.shape
    peers_step = 4 if n_seq % 4 == 0 else 1
    rows = per * BLOCK + extra
    return pl.pallas_call(
        functools.partial(pack_kernel, per, peers_step, extra),
        grid_spec=pltpu.PrefetchScalarGridSpec(
            num_scalar_prefetch=2,
            grid=(n_seq // peers_step,),
            in_specs=[pl.BlockSpec((blocks, BLOCK, cols), lambda i, s, a: (0, 0, 0))],
            out_specs=pl.BlockSpec((peers_step, rows, cols), lambda i, s, a: (i, 0, 0)),
        ),
        out_shape=jax.ShapeDtypeStruct((n_seq, rows, cols), BF16),
        compiler_params=params(PACK_LIMIT),
        cost_estimate=cost(0, 2 * 2 * n_seq * rows * cols),
    )(source, asked, tiles)


def seq_exchange(x):
    return lax.all_to_all(x, "seq", split_axis=0, concat_axis=0, tiled=True)


def head_pairs(step, swap):
    n_head = lax.axis_size("head")
    return [(h, (h + 2 * step) % n_head ^ swap) for h in range(n_head)]


def places_from(n_head):
    return [(step, swap) for step in range(n_head // 2) for swap in range(2)]


def head_gather(x):
    n_head = lax.axis_size("head")
    rounds = n_head // 2
    half = x.shape[0] // 2
    found = {0: [x]}
    up = down = x
    for step in range(1, rounds // 2 + 1):
        if 2 * step < rounds:
            up = lax.ppermute(up, "head", head_pairs(1, 0))
            down = lax.ppermute(down, "head", head_pairs(-1, 0))
            found[step], found[rounds - step] = [up], [down]
        else:
            found[step] = [
                lax.ppermute(up[:half], "head", head_pairs(1, 0)),
                lax.ppermute(down[half:], "head", head_pairs(-1, 0)),
            ]
    pieces = {}
    for step, blocks in found.items():
        pieces[step, 0] = blocks
        pieces[step, 1] = [lax.ppermute(b, "head", head_pairs(0, 1)) for b in blocks]
    return pieces


def head_send(chunks):
    order = places_from(lax.axis_size("head"))
    return [
        c if place == (0, 0) else lax.ppermute(c, "head", head_pairs(*place))
        for place, c in zip(order, chunks)
    ]


def shards(node_input, w_query, w_key, w_value, grad_context, key_blocks, counts):
    n_seq = lax.axis_size("seq")
    n_head = lax.axis_size("head")
    me = lax.axis_index("head")
    cols = w_query.shape[1]
    heads = cols // HDIM
    blocks = key_blocks.shape[0]
    nodes = blocks * BLOCK
    per = max(2, 3 * blocks * (KB - 1) // (2 * n_seq) + 1)
    slots = n_seq * per
    key_mask = head_mask(cols, SCALE)
    mask = head_mask(cols, 1.0)
    order = places_from(n_head)
    steps = jnp.array([p[0] for p in order], jnp.int32)
    swaps = jnp.array([p[1] for p in order], jnp.int32)
    targets = (lax.rem(me // 2 + steps, n_head // 2) * 2) + (lax.rem(me, 2) + swaps) % 2
    sources = (lax.rem(me // 2 - steps + n_head // 2, n_head // 2) * 2) + (lax.rem(me, 2) + swaps) % 2

    remote = key_blocks[:, 1:].reshape(-1)
    entries = remote.shape[0]
    owner = remote // blocks
    inner = remote % blocks
    numbers = jnp.arange(entries, dtype=jnp.int32)
    live = (numbers % (KB - 1)) + 1 < counts[numbers // (KB - 1)]
    before = (owner[:, None] == owner[None, :]) & (numbers[None, :] < numbers[:, None])
    slot_of = owner * per + jnp.sum(before.astype(jnp.int32), axis=1)
    taken = slot_of[None, :] == jnp.arange(slots, dtype=jnp.int32)[:, None]
    source = jnp.sum(jnp.where(taken, numbers[None, :] // (KB - 1), 0), axis=1)
    asked = jnp.sum(jnp.where(taken & live[None, :], inner[None, :] + 1, 0), axis=1) - 1
    upstream = lax.all_to_all(grad_context, "head", split_axis=1, concat_axis=0, tiled=True)
    grad_tiles = upstream.reshape(blocks, BLOCK, cols)
    far_grads = seq_exchange(pack(grad_tiles, source, asked, n_seq, per, 16))
    far_meta = far_grads[:, per * BLOCK : per * BLOCK + per, 0].astype(jnp.int32).reshape(-1)
    slot_numbers = jnp.arange(slots, dtype=jnp.int32)
    wanted = far_meta >= 0
    ahead = wanted[None, :] & (slot_numbers[None, :] < slot_numbers[:, None])
    rank = jnp.where(wanted, jnp.sum(ahead.astype(jnp.int32), axis=1), slots)
    far_order = jnp.sum(
        jnp.where(rank[None, :] == slot_numbers[:, None], slot_numbers[None, :], 0), axis=1
    )
    far_count = jnp.sum(wanted.astype(jnp.int32)).reshape(1)
    far_list = (far_count, far_order, far_meta)

    width = node_input.shape[1]
    found = head_gather(node_input)
    places, pieces = [], []
    for i, place in enumerate(order):
        for half, piece in enumerate(found[place]):
            places.append((i, None if len(found[place]) == 1 else half))
            pieces.append(piece)
    queries = pl.pallas_call(
        functools.partial(query_kernel, places),
        out_shape=jax.ShapeDtypeStruct((nodes, cols), BF16),
        in_specs=[SMEM] + [VMEM] * (len(pieces) + 1),
        out_specs=VMEM,
        compiler_params=params(ROWS_LIMIT),
        cost_estimate=cost(2 * nodes * width * cols, 2 * nodes * width),
    )(sources, *pieces, w_query)
    query_tiles = queries.reshape(blocks, BLOCK, cols)
    packed = pack(query_tiles, source, asked, n_seq, per, 0)
    far_queries = seq_exchange(packed)
    w_kv = jnp.concatenate([w_key, w_value], axis=1)
    packed, *pieces = lax.optimization_barrier((packed, *pieces))
    kv, gathered = pl.pallas_call(
        functools.partial(project_kernel, places),
        out_shape=(
            jax.ShapeDtypeStruct((nodes, 2 * cols), BF16),
            jax.ShapeDtypeStruct((nodes, width), BF16),
        ),
        in_specs=[SMEM] + [VMEM] * (len(pieces) + 1),
        out_specs=(VMEM,) * 2,
        compiler_params=params(ROWS_LIMIT),
        cost_estimate=cost(4 * nodes * width * cols, 4 * nodes * width),
    )(sources, *pieces, w_kv)

    w_all = jnp.concatenate([w_query, w_key, w_value], axis=1)
    w_all, _ = lax.optimization_barrier((w_all, kv))
    found = head_gather(w_all)
    halves = [len(found[place]) for place in order]
    w_pieces = [piece for place in order for piece in found[place]]
    far_queries, *w_pieces = lax.optimization_barrier((far_queries, *w_pieces))
    unit_flops = 2 * heads * BLOCK * BLOCK * cols
    tile_bytes = 2 * BLOCK * cols
    stats_shape = jax.ShapeDtypeStruct((slots, 2 * heads, BLOCK), F32)
    own_stats = pl.pallas_call(
        own_stats_kernel,
        out_shape=jax.ShapeDtypeStruct((blocks, 2 * heads, BLOCK), F32),
        in_specs=[VMEM] * 5,
        out_specs=VMEM,
        compiler_params=params(ATTEND_LIMIT),
        cost_estimate=cost(2 * blocks * unit_flops, 4 * blocks * tile_bytes),
    )(query_tiles, grad_tiles, kv, key_mask, mask)
    far_stats = pl.pallas_call(
        functools.partial(remote_stats_kernel, per),
        out_shape=stats_shape,
        in_specs=[SMEM] * 3 + [VMEM] * 5,
        out_specs=VMEM,
        compiler_params=params(ATTEND_LIMIT),
        cost_estimate=cost(2 * slots * unit_flops, 2 * slots * tile_bytes),
    )(*far_list, far_queries, far_grads, kv, key_mask, mask)
    row_stats_all, back = pl.pallas_call(
        merge_kernel,
        out_shape=(jax.ShapeDtypeStruct((blocks, 2 * heads, BLOCK), F32), stats_shape),
        in_specs=[SMEM, SMEM, VMEM, VMEM],
        out_specs=(VMEM, VMEM),
        scratch_shapes=[pltpu.VMEM((KB - 1, blocks, heads, BLOCK), F32)] * 2,
        compiler_params=params(ATTEND_LIMIT),
        cost_estimate=cost(0, 2 * 2 * slots * 4 * heads * BLOCK),
    )(slot_of, counts, own_stats, seq_exchange(far_stats))
    back = seq_exchange(back)

    far_terms = pl.pallas_call(
        functools.partial(far_query_kernel, per),
        out_shape=jax.ShapeDtypeStruct((slots, BLOCK, cols), BF16),
        in_specs=[SMEM] * 3 + [VMEM] * 6,
        out_specs=VMEM,
        compiler_params=params(ATTEND_LIMIT),
        cost_estimate=cost(3 * slots * unit_flops, 3 * slots * tile_bytes),
    )(
        *far_list,
        far_queries,
        far_grads,
        back,
        kv,
        key_mask,
        mask,
    )
    back_terms = seq_exchange(far_terms)

    rows = nodes // n_head
    tile_shape = (blocks, BLOCK, cols)
    own_terms, grad_key_value, *chunks = pl.pallas_call(
        functools.partial(key_value_kernel, per),
        out_shape=(
            jax.ShapeDtypeStruct(tile_shape, F32),
            jax.ShapeDtypeStruct((nodes, 2 * cols), BF16),
        )
        + (jax.ShapeDtypeStruct((rows, 2 * cols), BF16),) * n_head,
        in_specs=[SMEM] * 4 + [VMEM] * 9,
        out_specs=(VMEM,) * (2 + n_head),
        scratch_shapes=[
            pltpu.VMEM(tile_shape, F32),
            pltpu.VMEM(tile_shape, F32),
        ],
        compiler_params=params(ATTEND_LIMIT),
        cost_estimate=cost(5 * slots * unit_flops, 3 * slots * tile_bytes),
    )(
        targets,
        *far_list,
        far_queries,
        far_grads,
        back,
        query_tiles,
        grad_tiles,
        row_stats_all,
        kv,
        key_mask,
        mask,
    )

    grad_key_value, *w_pieces = lax.optimization_barrier((grad_key_value, *w_pieces))
    w_rows, w_kv_rows = pl.pallas_call(
        functools.partial(weights_kernel, halves),
        out_shape=(
            jax.ShapeDtypeStruct((width, n_head * cols), BF16),
            jax.ShapeDtypeStruct((width, n_head * 2 * cols), BF16),
        ),
        in_specs=[VMEM] * len(w_pieces),
        out_specs=(VMEM,) * 2,
        compiler_params=params(ROWS_LIMIT),
        cost_estimate=cost(0, 12 * width * n_head * cols),
    )(*w_pieces)
    contract_rows = (((0,), (0,)), ((), ()))
    chunks = head_send(chunks)
    term_key_value = lax.dot_general(gathered, grad_key_value, contract_rows, preferred_element_type=F32)
    back_terms, w_rows, w_kv_rows, *chunks = lax.optimization_barrier(
        (back_terms, w_rows, w_kv_rows, *chunks)
    )
    summed = pl.pallas_call(
        functools.partial(rows_kernel, n_head),
        out_shape=jax.ShapeDtypeStruct((rows, width), F32),
        in_specs=[VMEM] * (n_head + 1),
        out_specs=VMEM,
        compiler_params=params(TAIL_LIMIT),
        cost_estimate=cost(2 * rows * width * 2 * cols * n_head, 2 * width * 2 * cols * n_head),
    )(*chunks, w_kv_rows)

    grad_query, *chunks = pl.pallas_call(
        query_sum_kernel,
        out_shape=(jax.ShapeDtypeStruct((nodes, cols), BF16),)
        + (jax.ShapeDtypeStruct((rows, cols), BF16),) * n_head,
        in_specs=[SMEM] * 3 + [VMEM] * 2,
        out_specs=(VMEM,) * (1 + n_head),
        compiler_params=params(TAIL_LIMIT),
        cost_estimate=cost(0, slots * tile_bytes),
    )(targets, slot_of, counts, own_terms, back_terms)
    term_query = lax.dot_general(gathered, grad_query, contract_rows, preferred_element_type=F32)
    weight_terms = jnp.concatenate([term_query, term_key_value], axis=1).astype(BF16)
    weight_terms = seq_exchange(weight_terms.reshape(n_seq, width // n_seq, 3 * cols))
    weight_grads = jnp.sum(weight_terms.astype(F32), axis=0)
    chunks = head_send(chunks)
    grad_input = pl.pallas_call(
        functools.partial(rows_kernel, n_head),
        out_shape=jax.ShapeDtypeStruct((rows, width), BF16),
        in_specs=[VMEM] * (n_head + 2),
        out_specs=VMEM,
        compiler_params=params(TAIL_LIMIT),
        cost_estimate=cost(2 * rows * width * cols * n_head, 2 * width * cols * n_head),
    )(*chunks, w_rows, summed)
    return (
        grad_input,
        weight_grads[:, :cols],
        weight_grads[:, cols : 2 * cols],
        weight_grads[:, 2 * cols :],
    )


def solution(mesh):
    placed = (
        P(("seq", "head"), None),
        P(None, "head"),
        P(None, "head"),
        P(None, "head"),
        P(("seq", "head"), None),
        P("seq", None),
        P("seq"),
    )
    return jax.shard_map(
        shards,
        mesh=mesh,
        in_specs=placed,
        out_specs=(P(("seq", "head"), None), P("seq", "head"), P("seq", "head"), P("seq", "head")),
        check_vma=False,
    )
```

```python
import functools

import jax
import jax.numpy as jnp
from jax import lax
from jax.experimental import pallas as pl
from jax.experimental.pallas import tpu as pltpu
from jax.sharding import PartitionSpec as P

HDIM = 64
BLOCK = 128
KB = 4
BF16 = jnp.bfloat16
F32 = jnp.float32
SCALE = HDIM ** (-0.5)
GROUP = 8
MIB = 1024 * 1024
PACK_LIMIT = 8 * MIB
ROWS_LIMIT = 24 * MIB
ATTEND_LIMIT = 28 * MIB
TAIL_LIMIT = 36 * MIB
VMEM = pl.BlockSpec(memory_space=pltpu.VMEM)
SMEM = pl.BlockSpec(memory_space=pltpu.SMEM)
NT = (((1,), (1,)), ((), ()))
TN = (((0,), (0,)), ((), ()))


def params(limit):
    return pltpu.CompilerParams(vmem_limit_bytes=limit)


def cost(flops, moved):
    return pl.CostEstimate(flops=int(flops), bytes_accessed=int(moved), transcendentals=0)


def head_mask(width, scale):
    heads = width // HDIM
    row_head = jnp.arange(heads * BLOCK)[:, None] // BLOCK
    col_head = jnp.arange(width)[None, :] // HDIM
    return jnp.where(row_head == col_head, scale, 0.0).astype(BF16)


def by_head(tile, mask_ref):
    heads = mask_ref.shape[0] // BLOCK
    return jnp.concatenate([tile] * heads, axis=0) * mask_ref[...]


def products(key_heads, value_heads, query, grad):
    heads = key_heads.shape[0] // BLOCK
    scores = lax.dot_general(key_heads, query, NT, preferred_element_type=F32)
    grad_probs = lax.dot_general(value_heads, grad, NT, preferred_element_type=F32)
    return scores.reshape(heads, BLOCK, BLOCK), grad_probs.reshape(heads, BLOCK, BLOCK)


def row_stats(scores, grad_probs):
    top = jnp.max(scores, axis=1, keepdims=True)
    unnorm = jnp.exp(scores - top)
    total = jnp.sum(unnorm, axis=1)
    weighted = jnp.sum(unnorm * grad_probs, axis=1)
    return top[:, 0] + jnp.log(total), weighted / total


def entry_grads(scores, grad_probs, stats):
    heads = scores.shape[0]
    probs = jnp.exp(scores - stats[:heads][:, None, :])
    grad_scores = probs * (grad_probs - stats[heads:][:, None, :])
    flat = (heads * BLOCK, BLOCK)
    return probs.astype(BF16).reshape(flat), grad_scores.astype(BF16).reshape(flat)


def group_of(blocks):
    return GROUP if blocks % GROUP == 0 else 1


def tile_rows(ref, block, part, width):
    return ref[pl.ds(pl.multiple_of(block * BLOCK, BLOCK), BLOCK), part * width : (part + 1) * width]


def slot_rows(ref, slot, per):
    return ref[slot // per, pl.ds(lax.rem(slot, per) * BLOCK, BLOCK), :]


def remote_stats_kernel(
    per,
    count_ref,
    order_ref,
    meta_ref,
    query_ref,
    grad_ref,
    kv_ref,
    key_mask_ref,
    mask_ref,
    out_ref,
):
    heads = mask_ref.shape[0] // BLOCK
    width = mask_ref.shape[1]
    out_ref[...] = jnp.zeros_like(out_ref)
    n = count_ref[0]

    def step(g, carry):
        picked = [order_ref[jnp.minimum(g * GROUP + u, n - 1)] for u in range(GROUP)]
        pairs = [
            products(
                by_head(tile_rows(kv_ref, meta_ref[slot], 0, width), key_mask_ref),
                by_head(tile_rows(kv_ref, meta_ref[slot], 1, width), mask_ref),
                slot_rows(query_ref, slot, per),
                slot_rows(grad_ref, slot, per),
            )
            for slot in picked
        ]
        for slot, pair in zip(picked, pairs):
            lse, delta = row_stats(*pair)
            out_ref[slot, 0:heads] = lse
            out_ref[slot, heads : 2 * heads] = delta
        return carry

    lax.fori_loop(0, pl.cdiv(n, GROUP), step, 0)


def own_stats_kernel(query_ref, grad_ref, kv_ref, key_mask_ref, mask_ref, out_ref):
    heads = mask_ref.shape[0] // BLOCK
    width = mask_ref.shape[1]
    blocks = query_ref.shape[0]
    group = group_of(blocks)

    def step(g, carry):
        picked = [g * group + u for u in range(group)]
        pairs = [
            products(
                by_head(tile_rows(kv_ref, b, 0, width), key_mask_ref),
                by_head(tile_rows(kv_ref, b, 1, width), mask_ref),
                query_ref[b],
                grad_ref[b],
            )
            for b in picked
        ]
        for b, pair in zip(picked, pairs):
            lse, delta = row_stats(*pair)
            out_ref[b, 0:heads] = lse
            out_ref[b, heads : 2 * heads] = delta
        return carry

    lax.fori_loop(0, blocks // group, step, 0)


def merge_kernel(slot_ref, count_ref, own_ref, far_ref, row_ref, back_ref, lse_ref, delta_ref):
    blocks = own_ref.shape[0]
    heads = own_ref.shape[1] // 2
    back_ref[...] = jnp.zeros_like(back_ref)
    for b in range(blocks):
        for j in range(KB - 1):
            live = count_ref[b] > j + 1
            stats = far_ref[slot_ref[b * (KB - 1) + j]]
            lse_ref[j, b] = jnp.where(live, stats[:heads], -1e30)
            delta_ref[j, b] = jnp.where(live, stats[heads:], 0.0)
    own = own_ref[...]
    lses = [own[:, :heads]] + [lse_ref[j] for j in range(KB - 1)]
    deltas = [own[:, heads:]] + [delta_ref[j] for j in range(KB - 1)]
    top = functools.reduce(jnp.maximum, lses)
    weights = [jnp.exp(v - top) for v in lses]
    total = sum(weights)
    row_ref[:, :heads] = top + jnp.log(total)
    row_ref[:, heads:] = sum(w * d for w, d in zip(weights, deltas)) / total
    for b in range(blocks):
        for j in range(KB - 1):
            back_ref[slot_ref[b * (KB - 1) + j]] = row_ref[b]


def pick_heads(stacked):
    width = stacked.shape[1]
    heads = width // HDIM
    col_head = lax.broadcasted_iota(jnp.int32, (BLOCK, width), 1) // HDIM
    picked = stacked[:BLOCK]
    for h in range(1, heads):
        picked = jnp.where(col_head == h, stacked[h * BLOCK : (h + 1) * BLOCK], picked)
    return picked


def far_query_kernel(
    per,
    count_ref,
    order_ref,
    meta_ref,
    query_ref,
    grad_ref,
    stats_ref,
    kv_ref,
    key_mask_ref,
    mask_ref,
    out_ref,
):
    n = count_ref[0]
    width = mask_ref.shape[1]

    def step(g, carry):
        picked = [order_ref[jnp.minimum(g * GROUP + u, n - 1)] for u in range(GROUP)]
        pairs = [
            products(
                by_head(tile_rows(kv_ref, meta_ref[slot], 0, width), key_mask_ref),
                by_head(tile_rows(kv_ref, meta_ref[slot], 1, width), mask_ref),
                slot_rows(query_ref, slot, per),
                slot_rows(grad_ref, slot, per),
            )
            for slot in picked
        ]
        grads = [entry_grads(*pair, stats_ref[slot])[1] for slot, pair in zip(picked, pairs)]
        for slot, grad_scores in zip(picked, grads):
            key_heads = by_head(tile_rows(kv_ref, meta_ref[slot], 0, width), key_mask_ref)
            term = lax.dot_general(grad_scores, key_heads, TN, preferred_element_type=F32)
            out_ref[slot] = term.astype(BF16)
        return carry

    lax.fori_loop(0, pl.cdiv(n, GROUP), step, 0)


def key_value_kernel(
    per,
    target_ref,
    count_ref,
    order_ref,
    meta_ref,
    far_query_ref,
    far_grad_ref,
    far_stats_ref,
    query_ref,
    grad_ref,
    stats_ref,
    kv_ref,
    key_mask_ref,
    mask_ref,
    own_term_ref,
    out_ref,
    *rest,
):
    chunk_refs, (key_sum, value_sum) = rest[:-2], rest[-2:]
    blocks = query_ref.shape[0]
    width = query_ref.shape[2]
    group = group_of(blocks)

    def own(g, carry):
        picked = [g * group + u for u in range(group)]
        pairs = [
            products(
                by_head(tile_rows(kv_ref, b, 0, width), key_mask_ref),
                by_head(tile_rows(kv_ref, b, 1, width), mask_ref),
                query_ref[b],
                grad_ref[b],
            )
            for b in picked
        ]
        grads = [entry_grads(*pair, stats_ref[b]) for b, pair in zip(picked, pairs)]
        for b, (probs, grad_scores) in zip(picked, grads):
            key_heads = by_head(tile_rows(kv_ref, b, 0, width), key_mask_ref)
            own_term_ref[b] = lax.dot_general(grad_scores, key_heads, TN, preferred_element_type=F32)
            key_sum[b] = pick_heads(jnp.dot(grad_scores, query_ref[b], preferred_element_type=F32))
            value_sum[b] = pick_heads(jnp.dot(probs, grad_ref[b], preferred_element_type=F32))
        return carry

    lax.fori_loop(0, blocks // group, own, 0)
    n = count_ref[0]

    def far(g, carry):
        places = [g * GROUP + u for u in range(GROUP)]
        picked = [order_ref[jnp.minimum(at, n - 1)] for at in places]
        tiles = [
            (slot_rows(far_query_ref, slot, per), slot_rows(far_grad_ref, slot, per)) for slot in picked
        ]
        pairs = [
            products(
                by_head(tile_rows(kv_ref, meta_ref[slot], 0, width), key_mask_ref),
                by_head(tile_rows(kv_ref, meta_ref[slot], 1, width), mask_ref),
                *tile,
            )
            for slot, tile in zip(picked, tiles)
        ]
        grads = [entry_grads(*pair, far_stats_ref[slot]) for slot, pair in zip(picked, pairs)]
        terms = [
            (
                pick_heads(jnp.dot(grad_scores, query, preferred_element_type=F32)),
                pick_heads(jnp.dot(probs, grad, preferred_element_type=F32)),
            )
            for (probs, grad_scores), (query, grad) in zip(grads, tiles)
        ]
        for at, slot, (key_term, value_term) in zip(places, picked, terms):
            block = meta_ref[slot]
            key_sum[block] += jnp.where(at < n, key_term, 0.0)
            value_sum[block] += jnp.where(at < n, value_term, 0.0)
        return carry

    lax.fori_loop(0, pl.cdiv(n, GROUP), far, 0)
    for b in range(blocks):
        rows = slice(b * BLOCK, (b + 1) * BLOCK)
        out_ref[rows, :width] = (key_sum[b] * SCALE).astype(BF16)
        out_ref[rows, width:] = value_sum[b].astype(BF16)
    copy_chunks(target_ref, out_ref, chunk_refs)


def copy_chunks(target_ref, out_ref, chunk_refs):
    for i, chunk_ref in enumerate(chunk_refs):
        rows = chunk_ref.shape[0]
        chunk_ref[...] = out_ref[pl.ds(pl.multiple_of(target_ref[i] * rows, BLOCK), rows), :]


def query_sum_kernel(target_ref, slot_ref, count_ref, own_ref, far_ref, out_ref, *chunk_refs):
    blocks = own_ref.shape[0]

    for b in range(blocks):
        total = own_ref[b]
        for j in range(KB - 1):
            term = far_ref[slot_ref[b * (KB - 1) + j]].astype(F32)
            total = total + jnp.where(count_ref[b] > j + 1, term, 0.0)
        out_ref[b * BLOCK : (b + 1) * BLOCK, :] = total.astype(BF16)
    copy_chunks(target_ref, out_ref, chunk_refs)


def rows_kernel(n, *refs):
    chunks = jnp.concatenate([ref[...] for ref in refs[:n]], axis=1)
    weight_ref, out_ref = refs[n], refs[-1]
    total = lax.dot_general(chunks, weight_ref[...], NT, preferred_element_type=F32)
    if len(refs) == n + 3:
        total = total + refs[n + 1][...]
    out_ref[...] = total.astype(out_ref.dtype)


def weights_kernel(halves, *refs):
    query_ref, kv_ref = refs[-2:]
    piece_refs = list(refs[:-2])
    width = query_ref.shape[1] // len(halves)
    for i, count in enumerate(halves):
        start = 0
        for _ in range(count):
            piece = piece_refs.pop(0)
            rows = slice(start, start + piece.shape[0])
            start += piece.shape[0]
            query_ref[rows, i * width : (i + 1) * width] = piece[:, :width]
            kv_ref[rows, 2 * i * width : 2 * (i + 1) * width] = piece[:, width:]


def spans(places, source_ref, refs):
    for i, (index, half) in enumerate(places):
        rows = refs[i].shape[0]
        start = source_ref[index] * (rows if half is None else 2 * rows) + (half or 0) * rows
        yield refs[i], pl.ds(pl.multiple_of(start, 64), rows)


def query_kernel(places, source_ref, *refs):
    weight_ref, out_ref = refs[len(places) :]
    for ref, span in spans(places, source_ref, refs):
        out_ref[span, :] = jnp.dot(
            ref[...], weight_ref[...], preferred_element_type=F32
        ).astype(BF16)


def project_kernel(places, source_ref, *refs):
    weight_ref, kv_ref, out_ref = refs[len(places) :]
    for ref, span in spans(places, source_ref, refs):
        out_ref[span, :] = ref[...]
        kv_ref[span, :] = jnp.dot(
            ref[...], weight_ref[...], preferred_element_type=F32
        ).astype(BF16)


def pack_kernel(per, peers_step, extra, source_ref, asked_ref, tile_ref, out_ref):
    first = pl.program_id(0) * peers_step
    for p in range(peers_step):
        at = (first + p) * per
        for r in range(per):
            out_ref[p, r * BLOCK : (r + 1) * BLOCK, :] = tile_ref[source_ref[at + r]]
        if extra:
            row = lax.broadcasted_iota(jnp.int32, (extra, out_ref.shape[2]), 0)
            meta = jnp.zeros(row.shape, F32)
            for r in range(per):
                meta = jnp.where(row == r, asked_ref[at + r].astype(F32), meta)
            out_ref[p, per * BLOCK :, :] = meta.astype(BF16)


def pack(tiles, source, asked, n_seq, per, extra):
    blocks, _, cols = tiles.shape
    peers_step = 4 if n_seq % 4 == 0 else 1
    rows = per * BLOCK + extra
    return pl.pallas_call(
        functools.partial(pack_kernel, per, peers_step, extra),
        grid_spec=pltpu.PrefetchScalarGridSpec(
            num_scalar_prefetch=2,
            grid=(n_seq // peers_step,),
            in_specs=[pl.BlockSpec((blocks, BLOCK, cols), lambda i, s, a: (0, 0, 0))],
            out_specs=pl.BlockSpec((peers_step, rows, cols), lambda i, s, a: (i, 0, 0)),
        ),
        out_shape=jax.ShapeDtypeStruct((n_seq, rows, cols), BF16),
        compiler_params=params(PACK_LIMIT),
        cost_estimate=cost(0, 2 * 2 * n_seq * rows * cols),
    )(source, asked, tiles)


def seq_exchange(x):
    return lax.all_to_all(x, "seq", split_axis=0, concat_axis=0, tiled=True)


def head_pairs(step, swap):
    n_head = lax.axis_size("head")
    return [(h, (h + 2 * step) % n_head ^ swap) for h in range(n_head)]


def places_from(n_head):
    return [(step, swap) for step in range(n_head // 2) for swap in range(2)]


def head_gather(x):
    n_head = lax.axis_size("head")
    rounds = n_head // 2
    half = x.shape[0] // 2
    found = {0: [x]}
    up = down = x
    for step in range(1, rounds // 2 + 1):
        if 2 * step < rounds:
            up = lax.ppermute(up, "head", head_pairs(1, 0))
            down = lax.ppermute(down, "head", head_pairs(-1, 0))
            found[step], found[rounds - step] = [up], [down]
        else:
            found[step] = [
                lax.ppermute(up[:half], "head", head_pairs(1, 0)),
                lax.ppermute(down[half:], "head", head_pairs(-1, 0)),
            ]
    pieces = {}
    for step, blocks in found.items():
        pieces[step, 0] = blocks
        pieces[step, 1] = [lax.ppermute(b, "head", head_pairs(0, 1)) for b in blocks]
    return pieces


def head_send(chunks):
    order = places_from(lax.axis_size("head"))
    return [
        c if place == (0, 0) else lax.ppermute(c, "head", head_pairs(*place))
        for place, c in zip(order, chunks)
    ]


def shards(node_input, w_query, w_key, w_value, grad_context, key_blocks, counts):
    n_seq = lax.axis_size("seq")
    n_head = lax.axis_size("head")
    me = lax.axis_index("head")
    cols = w_query.shape[1]
    heads = cols // HDIM
    blocks = key_blocks.shape[0]
    nodes = blocks * BLOCK
    per = max(2, 3 * blocks * (KB - 1) // (2 * n_seq) + 1)
    slots = n_seq * per
    key_mask = head_mask(cols, SCALE)
    mask = head_mask(cols, 1.0)
    order = places_from(n_head)
    steps = jnp.array([p[0] for p in order], jnp.int32)
    swaps = jnp.array([p[1] for p in order], jnp.int32)
    targets = (lax.rem(me // 2 + steps, n_head // 2) * 2) + (lax.rem(me, 2) + swaps) % 2
    sources = (lax.rem(me // 2 - steps + n_head // 2, n_head // 2) * 2) + (lax.rem(me, 2) + swaps) % 2

    remote = key_blocks[:, 1:].reshape(-1)
    entries = remote.shape[0]
    owner = remote // blocks
    inner = remote % blocks
    numbers = jnp.arange(entries, dtype=jnp.int32)
    live = (numbers % (KB - 1)) + 1 < counts[numbers // (KB - 1)]
    before = (owner[:, None] == owner[None, :]) & (numbers[None, :] < numbers[:, None])
    slot_of = owner * per + jnp.sum(before.astype(jnp.int32), axis=1)
    taken = slot_of[None, :] == jnp.arange(slots, dtype=jnp.int32)[:, None]
    source = jnp.sum(jnp.where(taken, numbers[None, :] // (KB - 1), 0), axis=1)
    asked = jnp.sum(jnp.where(taken & live[None, :], inner[None, :] + 1, 0), axis=1) - 1
    upstream = lax.all_to_all(grad_context, "head", split_axis=1, concat_axis=0, tiled=True)
    grad_tiles = upstream.reshape(blocks, BLOCK, cols)
    far_grads = seq_exchange(pack(grad_tiles, source, asked, n_seq, per, 16))
    far_meta = far_grads[:, per * BLOCK : per * BLOCK + per, 0].astype(jnp.int32).reshape(-1)
    slot_numbers = jnp.arange(slots, dtype=jnp.int32)
    wanted = far_meta >= 0
    ahead = wanted[None, :] & (slot_numbers[None, :] < slot_numbers[:, None])
    rank = jnp.where(wanted, jnp.sum(ahead.astype(jnp.int32), axis=1), slots)
    far_order = jnp.sum(
        jnp.where(rank[None, :] == slot_numbers[:, None], slot_numbers[None, :], 0), axis=1
    )
    far_count = jnp.sum(wanted.astype(jnp.int32)).reshape(1)
    far_list = (far_count, far_order, far_meta)

    width = node_input.shape[1]
    found = head_gather(node_input)
    places, pieces = [], []
    for i, place in enumerate(order):
        for half, piece in enumerate(found[place]):
            places.append((i, None if len(found[place]) == 1 else half))
            pieces.append(piece)
    queries = pl.pallas_call(
        functools.partial(query_kernel, places),
        out_shape=jax.ShapeDtypeStruct((nodes, cols), BF16),
        in_specs=[SMEM] + [VMEM] * (len(pieces) + 1),
        out_specs=VMEM,
        compiler_params=params(ROWS_LIMIT),
        cost_estimate=cost(2 * nodes * width * cols, 2 * nodes * width),
    )(sources, *pieces, w_query)
    query_tiles = queries.reshape(blocks, BLOCK, cols)
    packed = pack(query_tiles, source, asked, n_seq, per, 0)
    far_queries = seq_exchange(packed)
    w_kv = jnp.concatenate([w_key, w_value], axis=1)
    packed, *pieces = lax.optimization_barrier((packed, *pieces))
    kv, gathered = pl.pallas_call(
        functools.partial(project_kernel, places),
        out_shape=(
            jax.ShapeDtypeStruct((nodes, 2 * cols), BF16),
            jax.ShapeDtypeStruct((nodes, width), BF16),
        ),
        in_specs=[SMEM] + [VMEM] * (len(pieces) + 1),
        out_specs=(VMEM,) * 2,
        compiler_params=params(ROWS_LIMIT),
        cost_estimate=cost(4 * nodes * width * cols, 4 * nodes * width),
    )(sources, *pieces, w_kv)

    w_all = jnp.concatenate([w_query, w_key, w_value], axis=1)
    w_all, _ = lax.optimization_barrier((w_all, kv))
    found = head_gather(w_all)
    halves = [len(found[place]) for place in order]
    w_pieces = [piece for place in order for piece in found[place]]
    far_queries, *w_pieces = lax.optimization_barrier((far_queries, *w_pieces))
    unit_flops = 2 * heads * BLOCK * BLOCK * cols
    tile_bytes = 2 * BLOCK * cols
    stats_shape = jax.ShapeDtypeStruct((slots, 2 * heads, BLOCK), F32)
    own_stats = pl.pallas_call(
        own_stats_kernel,
        out_shape=jax.ShapeDtypeStruct((blocks, 2 * heads, BLOCK), F32),
        in_specs=[VMEM] * 5,
        out_specs=VMEM,
        compiler_params=params(ATTEND_LIMIT),
        cost_estimate=cost(2 * blocks * unit_flops, 4 * blocks * tile_bytes),
    )(query_tiles, grad_tiles, kv, key_mask, mask)
    far_stats = pl.pallas_call(
        functools.partial(remote_stats_kernel, per),
        out_shape=stats_shape,
        in_specs=[SMEM] * 3 + [VMEM] * 5,
        out_specs=VMEM,
        compiler_params=params(ATTEND_LIMIT),
        cost_estimate=cost(2 * slots * unit_flops, 2 * slots * tile_bytes),
    )(*far_list, far_queries, far_grads, kv, key_mask, mask)
    row_stats_all, back = pl.pallas_call(
        merge_kernel,
        out_shape=(jax.ShapeDtypeStruct((blocks, 2 * heads, BLOCK), F32), stats_shape),
        in_specs=[SMEM, SMEM, VMEM, VMEM],
        out_specs=(VMEM, VMEM),
        scratch_shapes=[pltpu.VMEM((KB - 1, blocks, heads, BLOCK), F32)] * 2,
        compiler_params=params(ATTEND_LIMIT),
        cost_estimate=cost(0, 2 * 2 * slots * 4 * heads * BLOCK),
    )(slot_of, counts, own_stats, seq_exchange(far_stats))
    back = seq_exchange(back)

    far_terms = pl.pallas_call(
        functools.partial(far_query_kernel, per),
        out_shape=jax.ShapeDtypeStruct((slots, BLOCK, cols), BF16),
        in_specs=[SMEM] * 3 + [VMEM] * 6,
        out_specs=VMEM,
        compiler_params=params(ATTEND_LIMIT),
        cost_estimate=cost(3 * slots * unit_flops, 3 * slots * tile_bytes),
    )(
        *far_list,
        far_queries,
        far_grads,
        back,
        kv,
        key_mask,
        mask,
    )
    back_terms = seq_exchange(far_terms)

    rows = nodes // n_head
    tile_shape = (blocks, BLOCK, cols)
    own_terms, grad_key_value, *chunks = pl.pallas_call(
        functools.partial(key_value_kernel, per),
        out_shape=(
            jax.ShapeDtypeStruct(tile_shape, F32),
            jax.ShapeDtypeStruct((nodes, 2 * cols), BF16),
        )
        + (jax.ShapeDtypeStruct((rows, 2 * cols), BF16),) * n_head,
        in_specs=[SMEM] * 4 + [VMEM] * 9,
        out_specs=(VMEM,) * (2 + n_head),
        scratch_shapes=[
            pltpu.VMEM(tile_shape, F32),
            pltpu.VMEM(tile_shape, F32),
        ],
        compiler_params=params(ATTEND_LIMIT),
        cost_estimate=cost(5 * slots * unit_flops, 3 * slots * tile_bytes),
    )(
        targets,
        *far_list,
        far_queries,
        far_grads,
        back,
        query_tiles,
        grad_tiles,
        row_stats_all,
        kv,
        key_mask,
        mask,
    )

    grad_key_value, *w_pieces = lax.optimization_barrier((grad_key_value, *w_pieces))
    w_rows, w_kv_rows = pl.pallas_call(
        functools.partial(weights_kernel, halves),
        out_shape=(
            jax.ShapeDtypeStruct((width, n_head * cols), BF16),
            jax.ShapeDtypeStruct((width, n_head * 2 * cols), BF16),
        ),
        in_specs=[VMEM] * len(w_pieces),
        out_specs=(VMEM,) * 2,
        compiler_params=params(ROWS_LIMIT),
        cost_estimate=cost(0, 12 * width * n_head * cols),
    )(*w_pieces)
    contract_rows = (((0,), (0,)), ((), ()))
    chunks = head_send(chunks)
    term_key_value = lax.dot_general(gathered, grad_key_value, contract_rows, preferred_element_type=F32)
    back_terms, w_rows, w_kv_rows, *chunks = lax.optimization_barrier(
        (back_terms, w_rows, w_kv_rows, *chunks)
    )
    summed = pl.pallas_call(
        functools.partial(rows_kernel, n_head),
        out_shape=jax.ShapeDtypeStruct((rows, width), F32),
        in_specs=[VMEM] * (n_head + 1),
        out_specs=VMEM,
        compiler_params=params(TAIL_LIMIT),
        cost_estimate=cost(2 * rows * width * 2 * cols * n_head, 2 * width * 2 * cols * n_head),
    )(*chunks, w_kv_rows)

    grad_query, *chunks = pl.pallas_call(
        query_sum_kernel,
        out_shape=(jax.ShapeDtypeStruct((nodes, cols), BF16),)
        + (jax.ShapeDtypeStruct((rows, cols), BF16),) * n_head,
        in_specs=[SMEM] * 3 + [VMEM] * 2,
        out_specs=(VMEM,) * (1 + n_head),
        compiler_params=params(ATTEND_LIMIT * 2),
        cost_estimate=cost(0, slots * tile_bytes),
    )(targets, slot_of, counts, own_terms, back_terms)
    term_query = lax.dot_general(gathered, grad_query, contract_rows, preferred_element_type=F32)
    weight_terms = jnp.concatenate([term_query, term_key_value], axis=1).astype(BF16)
    weight_terms = seq_exchange(weight_terms.reshape(n_seq, width // n_seq, 3 * cols))
    weight_grads = [
        jnp.sum(weight_terms[:, :, i * cols : (i + 1) * cols].astype(F32), axis=0) for i in range(3)
    ]
    chunks = head_send(chunks)
    grad_input = pl.pallas_call(
        functools.partial(rows_kernel, n_head),
        out_shape=jax.ShapeDtypeStruct((rows, width), BF16),
        in_specs=[VMEM] * (n_head + 2),
        out_specs=VMEM,
        compiler_params=params(TAIL_LIMIT),
        cost_estimate=cost(2 * rows * width * cols * n_head, 2 * width * cols * n_head),
    )(*chunks, w_rows, summed)
    return (
        grad_input,
        *weight_grads,
    )


def solution(mesh):
    placed = (
        P(("seq", "head"), None),
        P(None, "head"),
        P(None, "head"),
        P(None, "head"),
        P(("seq", "head"), None),
        P("seq", None),
        P("seq"),
    )
    return jax.shard_map(
        shards,
        mesh=mesh,
        in_specs=placed,
        out_specs=(P(("seq", "head"), None), P("seq", "head"), P("seq", "head"), P("seq", "head")),
        check_vma=False,
    )
```
